512 devices in a mesh: ctx: 128 (over z, y, core), rep: 4 (over x).
Axes of the slice: x: 4, y: 8, z: 8, core: 2. Of those that a mesh axis runs over, the one named last changes fastest.
Arguments:
- offsets: int32 [4, 17], P('rep'), may hold values from 0 to 32768, as said below
- pairs: int32 [4, 1280, 2], P('rep', 'ctx'), may hold values from 0 to 5, as said below
- pair_count: int32 [4, 128], P('rep', 'ctx'), may hold values from 2 to 10, as said below
- queries: bfloat16 [4, 32768, 1024], P('rep', 'ctx'), may hold values from -6 to 6
- keys: bfloat16 [4, 32768, 1024], P('rep', 'ctx'), may hold values from -6 to 6
- values: bfloat16 [4, 32768, 1024], P('rep', 'ctx'), may hold values from -6 to 6
- cotangent: bfloat16 [4, 32768, 1024], P('rep', 'ctx'), may hold values from -6 to 6
- alpha: float32 [8], replicated, may hold values from 0.5 to 2
Outputs:
- attended: bfloat16 [4, 32768, 1024], P('rep', 'ctx')
- grad_queries: bfloat16 [4, 32768, 1024], P('rep', 'ctx')
- grad_keys: bfloat16 [4, 32768, 1024], P('rep', 'ctx')
- grad_values: bfloat16 [4, 32768, 1024], P('rep', 'ctx')
- grad_alpha: float32 [8], replicated
The draws below stay inside these ranges and needn't reach their ends.
Inputs may be any that keep to these rules, and one draw needn't show every extreme that they name: Per batch: offsets start at 0, never fall and end at 32768; every user holds at most 16384 events, one holds exactly 16384; some users may be empty. `pairs`: rows c * 10 to (c + 1) * 10 - 1 belong to ctx device c. For each of the device's query blocks a (0 to 1, in order) they list (a, b) for every key block from the block holding the later of two rows, the first event of the user of the query block's first row and that first row plus 1 minus 512, up to the query block itself; b counts blocks from the first block of device c - 2. Entries past pair_count are zero. Every pair holding a row pair with mask 1 is listed. `pair_count`: the number of listed pairs of each device, at least one for each query block; some device lists 10.
All inputs are finite; a program needn't handle non-finite values.
Results may differ from the reference program's by a relative error of at most 0.0049.
Values may be sent and summed in bfloat16 or wider, within the bound.
A program may use at most 64 MiB of HBM per device.

```python
import math
import jax
import jax.numpy as jnp
from jax import lax

D = 1024
H = 8
BLOCK = 128
WINDOW = 512
USERS = 16
ROW_DEV = 256
BATCHES = 4
ROWS = 32768
MAX_LEN = 16384
DEPTH = 2
PAIRS = 10
N_CTX = 128


def user_offsets(key):
    other = ROWS - MAX_LEN
    cut_total = USERS - 2
    close_pairs = cut_total // 2
    single = cut_total - 2 * close_pairs

    def one_batch(batch_key):
        base_key, near_key, single_key, slot_key = jax.random.split(batch_key, 4)
        base = jax.random.randint(base_key, (close_pairs,), 0, other - WINDOW // 2 + 1, dtype=jnp.int32)
        near = base + jax.random.randint(near_key, (close_pairs,), 1, WINDOW // 2 + 1, dtype=jnp.int32)
        lone = jax.random.randint(single_key, (single,), 0, other + 1, dtype=jnp.int32)
        cuts = jnp.sort(jnp.concatenate([base, near, lone]))
        bounds = jnp.concatenate([jnp.zeros((1,), jnp.int32), cuts, jnp.full((1,), other, jnp.int32)])
        slot = jax.random.randint(slot_key, (), 0, USERS, dtype=jnp.int32)
        index = jnp.arange(USERS + 1, dtype=jnp.int32)
        lower = jnp.take(bounds, jnp.minimum(index, USERS - 1))
        upper = jnp.take(bounds, jnp.maximum(index - 1, 0)) + MAX_LEN
        return jnp.where(index <= slot, lower, upper)
    batch_keys = jax.vmap(lambda index: jax.random.fold_in(key, index + 100))(jnp.arange(BATCHES, dtype=jnp.int32))
    return jax.vmap(one_batch)(batch_keys)


def pair_table(offsets_one):
    per_device = ROW_DEV // BLOCK
    block_ids = jnp.arange(N_CTX * per_device, dtype=jnp.int32)
    first_rows = block_ids * BLOCK
    users = jnp.sum((offsets_one[None, :] <= first_rows[:, None]).astype(jnp.int32), axis=1) - 1
    start_rows = jnp.maximum(jnp.take(offsets_one, users), first_rows - WINDOW + 1)
    starts = start_rows // BLOCK
    counts = (block_ids - starts + 1).reshape(N_CTX, per_device)
    starts = starts.reshape(N_CTX, per_device)
    before = jnp.cumsum(counts, axis=1) - counts
    totals = jnp.sum(counts, axis=1)
    slots = jnp.arange(PAIRS, dtype=jnp.int32)
    which = jnp.sum((before[:, None, :] <= slots[None, :, None]).astype(jnp.int32), axis=2) - 1
    start_sel = jnp.take_along_axis(starts, which, axis=1)
    before_sel = jnp.take_along_axis(before, which, axis=1)
    key_block = start_sel + slots[None, :] - before_sel
    devices = jnp.arange(N_CTX, dtype=jnp.int32)[:, None]
    window_block = key_block - (devices - DEPTH) * per_device
    valid = slots[None, :] < totals[:, None]
    entries = jnp.stack([jnp.where(valid, which, 0), jnp.where(valid, window_block, 0)], axis=-1)
    return (entries.reshape(N_CTX * PAIRS, 2), totals)


def draw_offsets(key, part):
    return user_offsets(key)


def draw_pairs(key, part):
    offs = user_offsets(key)
    return jax.vmap(lambda row: pair_table(row)[0])(offs)


def draw_pair_count(key, part):
    offs = user_offsets(key)
    return jax.vmap(lambda row: pair_table(row)[1])(offs)


def steps_of(key, shape, cuts, smallest, top_value):
    loudness, own = 1.0, jax.random.fold_in(key, 6)
    for dim, shards_of in cuts:
        steps = jnp.exp(jax.random.uniform(jax.random.fold_in(own, dim), (shards_of,), jnp.float32, smallest / len(cuts), top_value / len(cuts)))
        loudness = loudness * jnp.repeat(steps, shape[dim] // shards_of).reshape([-1 if axis == dim else 1 for axis in range(len(shape))])
    return loudness


def gaussian(own_key, dims, scale, bound, shards=(), held_as=jnp.bfloat16):
    values = jax.random.normal(own_key, dims, jnp.float32) * scale
    if len(shards) > 0:
        values = steps_of(own_key, dims, shards, -0.22, 0.18) * values
    return jnp.clip(values, min=-bound, max=bound).astype(held_as)


def setup_inputs(seed: int = 0) -> dict:
    key_list = jax.random.split(jax.random.key(seed), 9)
    return {
        "offsets": draw_offsets(jax.random.fold_in(key_list[8], 71), 0),
        "pairs": draw_pairs(jax.random.fold_in(key_list[8], 71), 0),
        "pair_count": draw_pair_count(jax.random.fold_in(key_list[8], 71), 0),
        "queries": gaussian(key_list[3], (BATCHES, ROWS, D), 1.0, 6.0, ((0, 4), (1, 128))),
        "keys": gaussian(key_list[4], (BATCHES, ROWS, D), 1.0, 6.0, ((0, 4), (1, 128))),
        "values": gaussian(key_list[5], (BATCHES, ROWS, D), 1.0, 6.0, ((0, 4), (1, 128))),
        "cotangent": gaussian(key_list[6], (BATCHES, ROWS, D), 1.0, 6.0, ((0, 4), (1, 128))),
        "alpha": jnp.clip(jnp.exp(jax.random.uniform(key_list[7], (H,), jnp.float32, math.log(0.5), math.log(2.0))), 0.5, 2.0),
    }


def multiply(form, left, right):
    return jnp.einsum(form, left.astype(jnp.float32), right.astype(jnp.float32))

def user_index(offsets_one, row_ids):
    return lax.optimization_barrier(jnp.sum((offsets_one[None, :] <= row_ids[:, None]).astype(jnp.int32), axis=1)) - 1

def row_scale(offsets_one, users):
    lengths = offsets_one[1:] - offsets_one[:-1]
    labels = jnp.arange(lengths.shape[0], dtype=jnp.int32)
    counted = lax.optimization_barrier(jnp.sum(jnp.where(users[:, None] == labels[None, :], lengths[None, :], 0), axis=1))
    return lax.rsqrt(jnp.minimum(counted, WINDOW).astype(jnp.float32))

def add_block(total, first, term):
    current = lax.dynamic_slice_in_dim(total, first, term.shape[0], 0)
    return lax.dynamic_update_slice_in_dim(total, current + term, first, 0)

def pair_terms(query_blk, key_blk, value_blk, grad_blk, weight, alpha):
    heads = alpha.shape[0]
    block = query_blk.shape[0]
    coeff = 1.0 / math.sqrt(query_blk.shape[1] // heads)
    shaped_q = query_blk.reshape(block, heads, -1)
    shaped_k = key_blk.reshape(block, heads, -1)
    shaped_v = value_blk.reshape(block, heads, -1)
    shaped_g = grad_blk.reshape(block, heads, -1)
    raw = multiply('qhd,khd->hqk', shaped_q, shaped_k) * coeff
    scores = alpha[:, None, None] * raw
    sigma = jax.nn.sigmoid(scores)
    attend = (scores * sigma * weight[None]).astype(jnp.bfloat16)
    output = multiply('hqk,khd->qhd', attend, shaped_v).reshape(block, -1)
    grad_attend = multiply('qhd,khd->hqk', shaped_g, shaped_v)
    grad_value = multiply('hqk,qhd->khd', attend, shaped_g).reshape(block, -1)
    grad_scores = grad_attend * weight[None] * sigma * (1.0 + scores * (1.0 - sigma))
    grad_alpha = lax.optimization_barrier(jnp.sum(grad_scores * raw, axis=(1, 2)))
    grad_raw = (grad_scores * (alpha[:, None, None] * coeff)).astype(jnp.bfloat16)
    grad_query = multiply('hqk,khd->qhd', grad_raw, shaped_k).reshape(block, -1)
    grad_key = multiply('hqk,qhd->khd', grad_raw, shaped_q).reshape(block, -1)
    return (output, grad_query, grad_key, grad_value, grad_alpha)

def run_pairs(plist, count, queries_own, grads_own, keys_win, values_win, q_users, q_rows, q_scale, k_users, k_rows, alpha):
    rows, width = queries_own.shape
    span = keys_win.shape[0]

    def one_pair(index, carry):
        out_acc, dq_acc, dk_acc, dv_acc, da_acc = carry
        query_first = plist[index, 0] * BLOCK
        key_first = plist[index, 1] * BLOCK

        def take_query(array):
            return lax.dynamic_slice_in_dim(array, query_first, BLOCK, 0)

        def take_key(array):
            return lax.dynamic_slice_in_dim(array, key_first, BLOCK, 0)
        apart = take_query(q_rows)[:, None] - take_key(k_rows)[None, :]
        mask = (take_query(q_users)[:, None] == take_key(k_users)[None, :]) & (apart >= 0) & (apart < WINDOW)
        weight = jnp.where(mask, take_query(q_scale)[:, None], jnp.zeros((), jnp.float32))
        terms = pair_terms(take_query(queries_own), take_key(keys_win), take_key(values_win), take_query(grads_own), weight, alpha)
        out_acc = add_block(out_acc, query_first, terms[0])
        dq_acc = add_block(dq_acc, query_first, terms[1])
        dk_acc = add_block(dk_acc, key_first, terms[2])
        dv_acc = add_block(dv_acc, key_first, terms[3])
        return (out_acc, dq_acc, dk_acc, dv_acc, da_acc + terms[4])
    init = (jnp.zeros((rows, width), jnp.float32), jnp.zeros((rows, width), jnp.float32), jnp.zeros((span, width), jnp.float32), jnp.zeros((span, width), jnp.float32), jnp.zeros(alpha.shape, jnp.float32))
    return lax.fori_loop(0, count, one_pair, init)

def reference(offsets, pairs, pair_count, queries, keys, values, cotangent, alpha):
    span_rows = (DEPTH + 1) * ROW_DEV
    outs_att, outs_dq, outs_dk, outs_dv = ([], [], [], [])
    total_alpha = jnp.zeros(alpha.shape, jnp.float32)
    for batch in range(BATCHES):
        offsets_one = offsets[batch]
        padding = jnp.zeros((DEPTH * ROW_DEV, D), jnp.bfloat16)
        keys_pad = jnp.concatenate([padding, keys[batch]], axis=0)
        values_pad = jnp.concatenate([padding, values[batch]], axis=0)

        def per_device(carry, device):
            dk_all, dv_all, grad_sum = carry
            q_rows = device * ROW_DEV + jnp.arange(ROW_DEV, dtype=jnp.int32)
            k_rows = (device - DEPTH) * ROW_DEV + jnp.arange(span_rows, dtype=jnp.int32)
            q_users = user_index(offsets_one, q_rows)
            k_users = user_index(offsets_one, k_rows)
            q_scale = row_scale(offsets_one, q_users)
            first = (device * ROW_DEV).astype(jnp.int32)
            queries_own = lax.dynamic_slice_in_dim(queries[batch], first, ROW_DEV, 0)
            grads_own = lax.dynamic_slice_in_dim(cotangent[batch], first, ROW_DEV, 0)
            keys_win = lax.dynamic_slice_in_dim(keys_pad, first, span_rows, 0)
            values_win = lax.dynamic_slice_in_dim(values_pad, first, span_rows, 0)
            plist = lax.dynamic_slice_in_dim(pairs[batch], (device * PAIRS).astype(jnp.int32), PAIRS, 0)
            count = lax.dynamic_index_in_dim(pair_count[batch], device, 0, keepdims=False)
            out_acc, dq_acc, dk_acc, dv_acc, da_acc = run_pairs(plist, count, queries_own, grads_own, keys_win, values_win, q_users, q_rows, q_scale, k_users, k_rows, alpha)
            dk_all = add_block(dk_all, first, dk_acc)
            dv_all = add_block(dv_all, first, dv_acc)
            return ((dk_all, dv_all, grad_sum + da_acc), (out_acc.astype(jnp.bfloat16), dq_acc.astype(jnp.bfloat16)))
        init = (jnp.zeros(((N_CTX + DEPTH) * ROW_DEV, D), jnp.float32), jnp.zeros(((N_CTX + DEPTH) * ROW_DEV, D), jnp.float32), jnp.zeros(alpha.shape, jnp.float32))
        carry, stacked = lax.scan(per_device, init, jnp.arange(N_CTX, dtype=jnp.int32))
        outs_att.append(stacked[0].reshape(ROWS, D))
        outs_dq.append(stacked[1].reshape(ROWS, D))
        outs_dk.append(carry[0][DEPTH * ROW_DEV:].astype(jnp.bfloat16))
        outs_dv.append(carry[1][DEPTH * ROW_DEV:].astype(jnp.bfloat16))
        total_alpha = total_alpha + carry[2]
    return (jnp.stack(outs_att), jnp.stack(outs_dq), jnp.stack(outs_dk), jnp.stack(outs_dv), total_alpha)
```

```python
import math

import jax
import jax.numpy as jnp
from jax import lax
from jax.experimental import pallas as pl
from jax.experimental.pallas import tpu as pltpu
from jax.sharding import PartitionSpec as P

WINDOW = 512
HEAD = 128
STRIP = 32
AHEAD = 4
LINE = 8
MESH = pl.DeviceIdType.MESH


def row_facts(offsets_ref, users, rows):
    start = jnp.zeros_like(rows)
    end = jnp.full_like(rows, 1 << 30)
    for user in range(users + 1):
        bound = offsets_ref[0, user]
        begun = rows >= bound
        start = jnp.where(begun, bound, start)
        end = jnp.where(begun, end, jnp.minimum(end, bound))
    length = jnp.minimum(end - start, WINDOW)
    return jnp.maximum(start, rows - (WINDOW - 1)), lax.rsqrt(length.astype(jnp.float32))


def fill_weights(offsets_ref, users, first, rows, weights):
    span = (rows, rows)
    down = lax.broadcasted_iota(jnp.int32, span, 0)
    across = lax.broadcasted_iota(jnp.int32, span, 1)
    lo, scale = row_facts(offsets_ref, users, first + lax.broadcasted_iota(jnp.int32, (rows, 1), 0))
    for segment, shift in ((0, 0), (1, -2 * rows), (2, -rows)):
        key = first + shift + across
        mask = (key >= lo) & (key <= first + down)
        weights[0, segment] = jnp.where(mask, scale, 0.0)
    for segment, shift in ((0, 0), (1, 2 * rows), (2, rows)):
        query = first + shift + lax.broadcasted_iota(jnp.int32, (1, rows), 1)
        lo, scale = row_facts(offsets_ref, users, query)
        key = first + down
        mask = (key >= lo) & (key <= query)
        weights[1, segment] = jnp.where(mask, scale, 0.0)


def dot_nt(left, right):
    return lax.dot_general(left, right, (((1,), (1,)), ((), ())), preferred_element_type=jnp.float32)


def dot_nn(left, right):
    return jnp.dot(left, right, preferred_element_type=jnp.float32)


def kernel(
    size,
    heads,
    users,
    offsets_hbm,
    alpha_hbm,
    q_hbm,
    k_hbm,
    v_hbm,
    g_hbm,
    out_ref,
    dq_ref,
    dk_ref,
    dv_ref,
    sum_ref,
    offsets_ref,
    alpha_ref,
    own,
    far,
    near,
    da_ref,
    share,
    gathered,
    weights,
    raw_s,
    gw_s,
    w_s,
    gr_s,
    acc,
    load_sem,
    far_send,
    far_recv,
    near_send,
    near_recv,
    share_send,
    share_recv,
):
    rows = q_hbm.shape[1]
    coeff = 1.0 / math.sqrt(HEAD)
    me = lax.axis_index("ctx")
    core = lax.rem(me, 2)
    sibling = me + 1 - 2 * core
    ahead = lax.rem(me + 2, size)
    behind = lax.rem(me + size - 2, size)
    sources = ((k_hbm, v_hbm), (q_hbm, g_hbm))
    targets = (ahead, behind)
    results = ((out_ref, dq_ref), (dv_ref, dk_ref))

    def head_of(step, d):
        return lax.rem(step + d * (heads // 2), heads)

    def columns(head):
        return pl.ds(pl.multiple_of(head * HEAD, HEAD), HEAD)

    def far_copy(step, d, m):
        head = head_of(step, d)
        return pltpu.make_async_remote_copy(
            src_ref=sources[d][m].at[0, :, columns(head)],
            dst_ref=far.at[d, head, m],
            send_sem=far_send.at[d, head, m],
            recv_sem=far_recv.at[d, head, m],
            device_id={"ctx": targets[d]},
            device_id_type=MESH,
        )

    def near_copy(step, d, m, forwarded):
        head = head_of(step, d)
        source = far.at[d, head, m] if forwarded else sources[d][m].at[0, :, columns(head)]
        return pltpu.make_async_remote_copy(
            src_ref=source,
            dst_ref=near.at[d, head, m],
            send_sem=near_send.at[d, head, m],
            recv_sem=near_recv.at[d, head, m],
            device_id={"ctx": sibling},
            device_id_type=MESH,
        )

    rep = lax.axis_index("rep")
    pair_x = rep * 2 + core
    y, z = lax.rem(me // 2, LINE), me // (2 * LINE)
    places = (pair_x, y, z)

    def member(stage, n):
        if stage == 0:
            return {"ctx": me - core + lax.rem(n, 2), "rep": n // 2}
        return {"ctx": me + (n - places[stage]) * (2 if stage == 1 else 2 * LINE), "rep": rep}

    def share_copy(stage, hop, slot):
        return pltpu.make_async_remote_copy(
            src_ref=share.at[stage],
            dst_ref=gathered.at[stage, slot],
            send_sem=share_send.at[stage, hop],
            recv_sem=share_recv.at[stage, slot],
            device_id=member(stage, lax.rem(places[stage] + hop, LINE)),
            device_id_type=MESH,
        )

    def share_start(stage, value):
        share[stage] = value
        gathered[stage, places[stage]] = value
        for hop in range(1, LINE):
            share_copy(stage, hop, places[stage]).start()

    def share_finish(stage):
        for hop in range(1, LINE):
            share_copy(stage, hop, lax.rem(places[stage] + hop, LINE)).wait_recv()
        return jnp.sum(gathered[stage], axis=0)

    both = tuple((d, m) for d in range(2) for m in range(2))
    loads = [
        pltpu.make_async_copy(array.at[0], own.at[n], load_sem.at[n])
        for n, array in enumerate((q_hbm, g_hbm, k_hbm, v_hbm))
    ]
    facts = [
        pltpu.make_async_copy(offsets_hbm, offsets_ref, load_sem.at[4]),
        pltpu.make_async_copy(alpha_hbm, alpha_ref, load_sem.at[5]),
    ]
    for copy in facts:
        copy.start()
    barrier = pltpu.get_barrier_semaphore()
    for device in (ahead, behind, sibling):
        pl.semaphore_signal(barrier, inc=1, device_id={"ctx": device}, device_id_type=MESH)
    for stage in range(3):
        for hop in range(1, LINE):
            other = lax.rem(places[stage] + hop, LINE)
            pl.semaphore_signal(barrier, inc=1, device_id=member(stage, other), device_id_type=MESH)
    pl.semaphore_wait(barrier, 3 + 3 * (LINE - 1))

    for step in range(AHEAD):
        for d, m in both:
            far_copy(step, d, m).start()
    for copy in loads:
        copy.start()

    @pl.loop(0, heads)
    def _(step):
        for m in range(2):

            @pl.when(core == 0)
            def _():
                near_copy(step, 0, m, False).start()

            @pl.when(core == 1)
            def _():
                near_copy(step, 1, m, False).start()

    for copy in facts:
        copy.wait()
    fill_weights(offsets_ref, users, me * rows, rows, weights)
    lanes = lax.broadcasted_iota(jnp.int32, (STRIP, HEAD), 1)
    sublanes = lax.broadcasted_iota(jnp.int32, (STRIP, HEAD), 0)
    w_s[...] = jnp.zeros_like(w_s)
    gr_s[...] = jnp.zeros_like(gr_s)
    for copy in loads:
        copy.wait()

    def element(raw, gw, scale):
        half = raw * scale
        tanh = jnp.tanh(half)
        twice = 1.0 + tanh
        silu = half * twice
        return silu, gw * (twice + silu * (1.0 - tanh))

    def weigh(d, segment, at, silu, grad):
        weight = weights[d, segment, *at]
        w_s[d, segment, *at] = (silu * weight).astype(jnp.bfloat16)
        scaled = grad * weight
        gr_s[d, segment, *at] = scaled.astype(jnp.bfloat16)
        return scaled

    def fold(product):
        return jnp.sum(product.reshape(-1, 8, HEAD), axis=0)

    def own_rows(n, head):
        return own[n, :, columns(head)]

    middle = heads // 2 - 1

    @pl.loop(0, heads)
    def _(step):
        for d, m in both:
            far_copy(step, d, m).wait_recv()
        for m in range(2):

            @pl.when(core == 1)
            def _():
                near_copy(step, 0, m, True).start()

            @pl.when(core == 0)
            def _():
                near_copy(step, 1, m, True).start()

        @pl.when(step + AHEAD < heads)
        def _():
            for d, m in both:
                far_copy(step, d, m).wait_send()
            for d, m in both:
                far_copy(step + AHEAD, d, m).start()

        for stage in range(1, 3):

            @pl.when(step == middle + 1 + stage)
            def _():
                share_start(stage, share_finish(stage - 1))

        for d in range(2):
            head = head_of(step, d)
            r1, r2 = own_rows(2 * d, head), own_rows(2 * d + 1, head)
            raw_s[d, 0] = dot_nt(r1, own_rows(2 - 2 * d, head))
            raw_s[d, 1] = dot_nt(r1, far[d, head, 0])
            gw_s[d, 0] = dot_nt(r2, own_rows(3 - 2 * d, head))
            gw_s[d, 1] = dot_nt(r2, far[d, head, 1])
        for d in range(2):
            head = head_of(step, d)
            scale = 0.5 * coeff * alpha_ref[head]
            total = jnp.zeros((8, HEAD), jnp.float32)
            for row in range(0, rows, STRIP):
                for column in range(0, rows, HEAD):
                    at = (pl.ds(row, STRIP), pl.ds(column, HEAD))
                    if row // HEAD == column // HEAD:
                        gap = column - row + lanes - sublanes
                        mine = gap <= 0 if d == 0 else gap >= 0
                        raw = jnp.where(mine, raw_s[d, 0, *at], raw_s[d, 1, *at])
                        gw = jnp.where(mine, gw_s[d, 0, *at], gw_s[d, 1, *at])
                        silu, grad = element(raw, gw, scale)
                        total += fold((weigh(d, 0, at, silu, grad) + weigh(d, 1, at, silu, grad)) * raw)
                    else:
                        segment = int((row < column) == (d == 0))
                        raw = raw_s[d, segment, *at]
                        silu, grad = element(raw, gw_s[d, segment, *at], scale)
                        total += fold(weigh(d, segment, at, silu, grad) * raw)
            da_ref[d, step] = total * (0.5 * coeff)
            acc[d, 0] = dot_nn(w_s[d, 0], own_rows(3 - 2 * d, head)) + dot_nn(w_s[d, 1], far[d, head, 1])
            acc[d, 1] = dot_nn(gr_s[d, 0], own_rows(2 - 2 * d, head)) + dot_nn(gr_s[d, 1], far[d, head, 0])

        for d, m in both:
            near_copy(step, d, m, True).wait_recv()
        for d in range(2):
            head = head_of(step, d)
            raw_s[d, 2] = dot_nt(own_rows(2 * d, head), near[d, head, 0])
            gw_s[d, 2] = dot_nt(own_rows(2 * d + 1, head), near[d, head, 1])
        for d in range(2):
            head = head_of(step, d)
            scale = 0.5 * coeff * alpha_ref[head]
            total = jnp.zeros((8, HEAD), jnp.float32)
            for row in range(0, rows, STRIP):
                for column in range(0, rows, HEAD):
                    at = (pl.ds(row, STRIP), pl.ds(column, HEAD))
                    raw = raw_s[d, 2, *at]
                    silu, grad = element(raw, gw_s[d, 2, *at], scale)
                    total += fold(weigh(d, 2, at, silu, grad) * raw)
            da_ref[d, step] += total * (0.5 * coeff)
            first = acc[d, 0] + dot_nn(w_s[d, 2], near[d, head, 1])
            second = (acc[d, 1] + dot_nn(gr_s[d, 2], near[d, head, 0])) * scale
            results[d][0][0, :, columns(head)] = first.astype(jnp.bfloat16)
            results[d][1][0, :, columns(head)] = second.astype(jnp.bfloat16)

        @pl.when(step == middle)
        def _():
            for d in range(2):
                half = pl.ds(d * (heads // 2), heads // 2)
                share[0, half] = jnp.sum(da_ref[d, pl.ds(0, heads // 2)], axis=1)
            share_start(0, share[0])

    @pl.loop(0, heads)
    def _(step):
        for d, m in both:

            @pl.when(step + AHEAD >= heads)
            def _():
                far_copy(step, d, m).wait_send()

            near_copy(step, d, m, True).wait_send()

    sum_ref[...] = share_finish(2)
    for stage in range(3):
        for hop in range(1, LINE):
            share_copy(stage, hop, places[stage]).wait_send()


def shards(offsets, pairs, pair_count, queries, keys, values, cotangent, alpha):
    rows, width = queries.shape[1:]
    heads = alpha.shape[0]
    size = lax.axis_size("ctx")
    anywhere = pl.BlockSpec(memory_space=pl.ANY)

    def body(*refs):
        kernel(size, heads, offsets.shape[1] - 1, *refs)

    inputs = (offsets, alpha, queries, keys, values, cotangent)
    in_vmem = pltpu.VMEM((1, rows, width), jnp.bfloat16)
    *results, total = pl.pallas_call(
        body,
        out_shape=(in_vmem,) * 4 + (pltpu.VMEM((heads, HEAD), jnp.float32),),
        in_specs=[anywhere] * 6,
        out_specs=[pl.BlockSpec(memory_space=pltpu.VMEM)] * 5,
        scratch_shapes=[
            pltpu.SMEM(offsets.shape, jnp.int32),
            pltpu.SMEM(alpha.shape, jnp.float32),
            pltpu.VMEM((4, rows, width), jnp.bfloat16),
            pltpu.VMEM((2, heads, 2, rows, HEAD), jnp.bfloat16),
            pltpu.VMEM((2, heads, 2, rows, HEAD), jnp.bfloat16),
            pltpu.VMEM((2, heads, 8, HEAD), jnp.float32),
            pltpu.VMEM((3, heads, HEAD), jnp.float32),
            pltpu.VMEM((3, LINE, heads, HEAD), jnp.float32),
            pltpu.VMEM((2, 3, rows, rows), jnp.float32),
            pltpu.VMEM((2, 3, rows, rows), jnp.float32),
            pltpu.VMEM((2, 3, rows, rows), jnp.float32),
            pltpu.VMEM((2, 3, rows, rows), jnp.bfloat16),
            pltpu.VMEM((2, 3, rows, rows), jnp.bfloat16),
            pltpu.VMEM((2, 2, rows, HEAD), jnp.float32),
            pltpu.SemaphoreType.DMA((6,)),
            pltpu.SemaphoreType.DMA((2, heads, 2)),
            pltpu.SemaphoreType.DMA((2, heads, 2)),
            pltpu.SemaphoreType.DMA((2, heads, 2)),
            pltpu.SemaphoreType.DMA((2, heads, 2)),
            pltpu.SemaphoreType.DMA((3, LINE)),
            pltpu.SemaphoreType.DMA((3, LINE)),
        ],
        compiler_params=pltpu.CompilerParams(
            collective_id=0, has_side_effects=True, vmem_limit_bytes=40 * 1024 * 1024
        ),
        cost_estimate=pl.CostEstimate(
            flops=48 * heads * rows * rows * HEAD,
            bytes_accessed=8 * rows * width,
            transcendentals=4 * heads * rows * rows,
        ),
    )(*(pltpu.with_memory_space_constraint(array, pltpu.HBM) for array in inputs))
    return (*results, jnp.sum(total, axis=1))


def solution(mesh):
    return jax.shard_map(
        shards,
        mesh=mesh,
        in_specs=(
            P("rep", None),
            P("rep", "ctx", None),
            P("rep", "ctx"),
            P("rep", "ctx", None),
            P("rep", "ctx", None),
            P("rep", "ctx", None),
            P("rep", "ctx", None),
            P(),
        ),
        out_specs=(
            P("rep", "ctx", None),
            P("rep", "ctx", None),
            P("rep", "ctx", None),
            P("rep", "ctx", None),
            P(),
        ),
        check_vma=False,
    )
```

```python
import math

import jax
import jax.numpy as jnp
from jax import lax
from jax.experimental import pallas as pl
from jax.experimental.pallas import tpu as pltpu
from jax.sharding import PartitionSpec as P

WINDOW = 512
HEAD = 128
STRIP = 32
AHEAD = 2
LINE = 8
MESH = pl.DeviceIdType.MESH


def row_facts(offsets_ref, users, rows):
    start = jnp.zeros_like(rows)
    end = jnp.full_like(rows, 1 << 30)
    for user in range(users + 1):
        bound = offsets_ref[0, user]
        begun = rows >= bound
        start = jnp.where(begun, bound, start)
        end = jnp.where(begun, end, jnp.minimum(end, bound))
    length = jnp.minimum(end - start, WINDOW)
    return jnp.maximum(start, rows - (WINDOW - 1)), lax.rsqrt(length.astype(jnp.float32))


def fill_weights(offsets_ref, users, first, rows, weights):
    span = (rows, rows)
    down = lax.broadcasted_iota(jnp.int32, span, 0)
    across = lax.broadcasted_iota(jnp.int32, span, 1)
    lo, scale = row_facts(offsets_ref, users, first + lax.broadcasted_iota(jnp.int32, (rows, 1), 0))
    for segment, shift in ((0, 0), (1, -2 * rows), (2, -rows)):
        key = first + shift + across
        mask = (key >= lo) & (key <= first + down)
        weights[0, segment] = jnp.where(mask, scale, 0.0)
    for segment, shift in ((0, 0), (1, 2 * rows), (2, rows)):
        query = first + shift + lax.broadcasted_iota(jnp.int32, (1, rows), 1)
        lo, scale = row_facts(offsets_ref, users, query)
        key = first + down
        mask = (key >= lo) & (key <= query)
        weights[1, segment] = jnp.where(mask, scale, 0.0)


def dot_nt(left, right):
    return lax.dot_general(left, right, (((1,), (1,)), ((), ())), preferred_element_type=jnp.float32)


def dot_nn(left, right):
    return jnp.dot(left, right, preferred_element_type=jnp.float32)


def kernel(
    size,
    heads,
    users,
    offsets_hbm,
    alpha_hbm,
    q_hbm,
    k_hbm,
    v_hbm,
    g_hbm,
    out_ref,
    dq_ref,
    dk_ref,
    dv_ref,
    sum_ref,
    offsets_ref,
    alpha_ref,
    own,
    far,
    near,
    da_ref,
    share,
    gathered,
    weights,
    raw_s,
    gw_s,
    w_s,
    gr_s,
    acc,
    load_sem,
    far_send,
    far_recv,
    near_send,
    near_recv,
    share_send,
    share_recv,
    reached,
):
    rows = q_hbm.shape[1]
    coeff = 1.0 / math.sqrt(HEAD)
    me = lax.axis_index("ctx")
    core = lax.rem(me, 2)
    sibling = me + 1 - 2 * core
    ahead, behind = jnp.minimum(me + 2, size - 1), jnp.maximum(me - 2, 0)
    has_ahead, has_behind = me < size - 2, me >= 2
    sources = ((k_hbm, v_hbm), (q_hbm, g_hbm))
    targets = (ahead, behind)
    sends, receives = (has_ahead, has_behind), (has_behind, has_ahead)
    direct = (core == 0, core == 1)
    relays = ((core == 1) & has_behind, (core == 0) & has_ahead)
    near_sends = (me != 1, me != size - 2)
    near_receives = (me != 0, me != size - 1)
    results = ((out_ref, dq_ref), (dv_ref, dk_ref))

    def head_of(step, d):
        return lax.rem(step + d * (heads // 2), heads)

    def columns(head):
        return pl.ds(pl.multiple_of(head * HEAD, HEAD), HEAD)

    def far_copy(step, d, m):
        head = head_of(step, d)
        return pltpu.make_async_remote_copy(
            src_ref=sources[d][m].at[0, :, columns(head)],
            dst_ref=far.at[d, head, m],
            send_sem=far_send.at[d, head, m],
            recv_sem=far_recv.at[d, head, m],
            device_id={"ctx": targets[d]},
            device_id_type=MESH,
        )

    def near_copy(step, d, m, forwarded):
        head = head_of(step, d)
        source = far.at[d, head, m] if forwarded else sources[d][m].at[0, :, columns(head)]
        return pltpu.make_async_remote_copy(
            src_ref=source,
            dst_ref=near.at[d, head, m],
            send_sem=near_send.at[d, head, m],
            recv_sem=near_recv.at[d, head, m],
            device_id={"ctx": sibling},
            device_id_type=MESH,
        )

    rep = lax.axis_index("rep")
    pair_x = rep * 2 + core
    y, z = lax.rem(me // 2, LINE), me // (2 * LINE)
    places = (pair_x, y, z)

    def member(stage, n):
        if stage == 0:
            return {"ctx": me - core + lax.rem(n, 2), "rep": n // 2}
        return {"ctx": me + (n - places[stage]) * (2 if stage == 1 else 2 * LINE), "rep": rep}

    def share_copy(stage, hop, slot):
        return pltpu.make_async_remote_copy(
            src_ref=share.at[stage],
            dst_ref=gathered.at[stage, slot],
            send_sem=share_send.at[stage, hop],
            recv_sem=share_recv.at[stage, slot],
            device_id=member(stage, lax.rem(places[stage] + hop, LINE)),
            device_id_type=MESH,
        )

    def share_start(stage, value):
        share[stage] = value
        gathered[stage, places[stage]] = value
        for hop in range(1, LINE):
            share_copy(stage, hop, places[stage]).start()

    def share_finish(stage):
        for hop in range(1, LINE):
            share_copy(stage, hop, lax.rem(places[stage] + hop, LINE)).wait_recv()
        return jnp.sum(gathered[stage], axis=0)

    loads = [
        pltpu.make_async_copy(array.at[0], own.at[n], load_sem.at[n])
        for n, array in enumerate((q_hbm, g_hbm, k_hbm, v_hbm))
    ]
    facts = [
        pltpu.make_async_copy(offsets_hbm, offsets_ref, load_sem.at[4]),
        pltpu.make_async_copy(alpha_hbm, alpha_ref, load_sem.at[5]),
    ]
    for copy in facts:
        copy.start()
    def far_start(step):
        for d in range(2):

            @pl.when(sends[d])
            def _():
                for m in range(2):
                    far_copy(step, d, m).start()

    def near_start(step, conditions, forwarded):
        for d in range(2):

            @pl.when(conditions[d])
            def _():
                for m in range(2):
                    near_copy(step, d, m, forwarded).start()

    def wait_if(condition, *waits):
        @pl.when(condition)
        def _():
            for wait in waits:
                wait()

    barrier = pltpu.get_barrier_semaphore()

    def along_z(distance):
        inside = z + distance < LINE if distance > 0 else z + distance >= 0
        return inside, {"ctx": jnp.clip(me + 2 * LINE * distance, 0, size - 1)}

    def count(conditions):
        return sum(condition.astype(jnp.int32) for condition in conditions)

    greeted = [(has_ahead, {"ctx": ahead}), (has_behind, {"ctx": behind}), along_z(1), along_z(-1)]
    for exists, device in greeted:

        @pl.when(exists)
        def _():
            pl.semaphore_signal(barrier, inc=1, device_id=device, device_id_type=MESH)

    pl.semaphore_signal(barrier, inc=1, device_id={"ctx": sibling}, device_id_type=MESH)
    for stage in range(2):
        for hop in range(1, LINE):
            other = lax.rem(places[stage] + hop, LINE)
            pl.semaphore_signal(barrier, inc=1, device_id=member(stage, other), device_id_type=MESH)
    pl.semaphore_wait(barrier, 1 + 2 * (LINE - 1) + count([exists for exists, _ in greeted]))

    for step in range(AHEAD):
        far_start(step)
    for copy in loads:
        copy.start()
    for step in range(AHEAD):
        near_start(step, direct, False)

    def pass_on(n):
        for distance in (1 << n, -(1 << n)):
            exists, device = along_z(distance)

            @pl.when(exists)
            def _():
                pl.semaphore_signal(reached.at[n], inc=1, device_id=device, device_id_type=MESH)

    def learn(n):
        pl.semaphore_wait(reached.at[n], count([along_z(1 << n)[0], along_z(-(1 << n))[0]]))

    pass_on(0)
    for d in range(2):

        @pl.when(jnp.logical_not(receives[d]))
        def _():
            far[d] = jnp.zeros(far.shape[1:], far.dtype)

        @pl.when(jnp.logical_not(near_receives[d]))
        def _():
            near[d] = jnp.zeros(near.shape[1:], near.dtype)

    for copy in facts:
        copy.wait()
    fill_weights(offsets_ref, users, me * rows, rows, weights)
    lanes = lax.broadcasted_iota(jnp.int32, (STRIP, HEAD), 1)
    sublanes = lax.broadcasted_iota(jnp.int32, (STRIP, HEAD), 0)
    w_s[...] = jnp.zeros_like(w_s)
    gr_s[...] = jnp.zeros_like(gr_s)
    for copy in loads:
        copy.wait()

    def element(raw, gw, scale):
        half = raw * scale
        tanh = jnp.tanh(half)
        twice = 1.0 + tanh
        silu = half * twice
        return silu, gw * scale * (twice + silu * (1.0 - tanh))

    def weigh(d, segment, at, silu, grad):
        weight = weights[d, segment, *at]
        w_s[d, segment, *at] = (silu * weight).astype(jnp.bfloat16)
        scaled = grad * weight
        gr_s[d, segment, *at] = scaled.astype(jnp.bfloat16)
        return scaled

    def fold(product):
        return jnp.sum(product.reshape(-1, 8, HEAD), axis=0)

    def own_rows(n, head):
        return own[n, :, columns(head)]

    middle = heads // 2 - 1

    @pl.loop(0, heads)
    def _(step):
        for d in range(2):
            wait_if(receives[d], *(far_copy(step, d, m).wait_recv for m in range(2)))
        near_start(step, relays, True)

        @pl.when(step + AHEAD < heads)
        def _():
            for d in range(2):
                wait_if(sends[d], *(far_copy(step, d, m).wait_send for m in range(2)))
            far_start(step + AHEAD)
            near_start(step + AHEAD, direct, False)

        for n in range(2):

            @pl.when(step == 2 * n + 2)
            def _():
                learn(n)
                pass_on(n + 1)

        for stage in range(1, 3):

            @pl.when(step == heads - 3 + stage)
            def _():
                if stage == 2:
                    learn(2)
                share_start(stage, share_finish(stage - 1))

        for d in range(2):
            head = head_of(step, d)
            r1, r2 = own_rows(2 * d, head), own_rows(2 * d + 1, head)
            raw_s[d, 0] = dot_nt(r1, own_rows(2 - 2 * d, head))
            raw_s[d, 1] = dot_nt(r1, far[d, head, 0])
            gw_s[d, 0] = dot_nt(r2, own_rows(3 - 2 * d, head))
            gw_s[d, 1] = dot_nt(r2, far[d, head, 1])
        for d in range(2):
            head = head_of(step, d)
            scale = 0.5 * coeff * alpha_ref[head]
            total = jnp.zeros((8, HEAD), jnp.float32)
            for row in range(0, rows, STRIP):
                for column in range(0, rows, HEAD):
                    at = (pl.ds(row, STRIP), pl.ds(column, HEAD))
                    if row // HEAD == column // HEAD:
                        gap = column - row + lanes - sublanes
                        mine = gap <= 0 if d == 0 else gap >= 0
                        raw = jnp.where(mine, raw_s[d, 0, *at], raw_s[d, 1, *at])
                        gw = jnp.where(mine, gw_s[d, 0, *at], gw_s[d, 1, *at])
                        silu, grad = element(raw, gw, scale)
                        total += fold((weigh(d, 0, at, silu, grad) + weigh(d, 1, at, silu, grad)) * raw)
                    else:
                        segment = int((row < column) == (d == 0))
                        raw = raw_s[d, segment, *at]
                        silu, grad = element(raw, gw_s[d, segment, *at], scale)
                        total += fold(weigh(d, segment, at, silu, grad) * raw)
            da_ref[d, step] = total / alpha_ref[head]
            acc[d, 0] = dot_nn(w_s[d, 0], own_rows(3 - 2 * d, head)) + dot_nn(w_s[d, 1], far[d, head, 1])
            acc[d, 1] = dot_nn(gr_s[d, 0], own_rows(2 - 2 * d, head)) + dot_nn(gr_s[d, 1], far[d, head, 0])

        for d in range(2):
            wait_if(near_receives[d], *(near_copy(step, d, m, True).wait_recv for m in range(2)))
        for d in range(2):
            head = head_of(step, d)
            raw_s[d, 2] = dot_nt(own_rows(2 * d, head), near[d, head, 0])
            gw_s[d, 2] = dot_nt(own_rows(2 * d + 1, head), near[d, head, 1])
        for d in range(2):
            head = head_of(step, d)
            scale = 0.5 * coeff * alpha_ref[head]
            total = jnp.zeros((8, HEAD), jnp.float32)
            for row in range(0, rows, STRIP):
                for column in range(0, rows, HEAD):
                    at = (pl.ds(row, STRIP), pl.ds(column, HEAD))
                    raw = raw_s[d, 2, *at]
                    silu, grad = element(raw, gw_s[d, 2, *at], scale)
                    total += fold(weigh(d, 2, at, silu, grad) * raw)
            da_ref[d, step] += total / alpha_ref[head]
            first = acc[d, 0] + dot_nn(w_s[d, 2], near[d, head, 1])
            second = acc[d, 1] + dot_nn(gr_s[d, 2], near[d, head, 0])
            results[d][0][0, :, columns(head)] = first.astype(jnp.bfloat16)
            results[d][1][0, :, columns(head)] = second.astype(jnp.bfloat16)

        @pl.when(step == middle)
        def _():
            for d in range(2):
                half = pl.ds(d * (heads // 2), heads // 2)
                share[0, half] = jnp.sum(da_ref[d, pl.ds(0, heads // 2)], axis=1)
            share_start(0, share[0])

    @pl.loop(0, heads)
    def _(step):
        for d in range(2):
            wait_if(
                sends[d] & (step + AHEAD >= heads), *(far_copy(step, d, m).wait_send for m in range(2))
            )
            wait_if(near_sends[d], *(near_copy(step, d, m, True).wait_send for m in range(2)))

    sum_ref[...] = share_finish(2)
    for stage in range(3):
        for hop in range(1, LINE):
            share_copy(stage, hop, places[stage]).wait_send()


def shards(offsets, pairs, pair_count, queries, keys, values, cotangent, alpha):
    rows, width = queries.shape[1:]
    heads = alpha.shape[0]
    size = lax.axis_size("ctx")
    anywhere = pl.BlockSpec(memory_space=pl.ANY)

    def body(*refs):
        kernel(size, heads, offsets.shape[1] - 1, *refs)

    inputs = (offsets, alpha, queries, keys, values, cotangent)
    in_vmem = pltpu.VMEM((1, rows, width), jnp.bfloat16)
    *results, total = pl.pallas_call(
        body,
        out_shape=(in_vmem,) * 4 + (pltpu.VMEM((heads, HEAD), jnp.float32),),
        in_specs=[anywhere] * 6,
        out_specs=[pl.BlockSpec(memory_space=pltpu.VMEM)] * 5,
        scratch_shapes=[
            pltpu.SMEM(offsets.shape, jnp.int32),
            pltpu.SMEM(alpha.shape, jnp.float32),
            pltpu.VMEM((4, rows, width), jnp.bfloat16),
            pltpu.VMEM((2, heads, 2, rows, HEAD), jnp.bfloat16),
            pltpu.VMEM((2, heads, 2, rows, HEAD), jnp.bfloat16),
            pltpu.VMEM((2, heads, 8, HEAD), jnp.float32),
            pltpu.VMEM((3, heads, HEAD), jnp.float32),
            pltpu.VMEM((3, LINE, heads, HEAD), jnp.float32),
            pltpu.VMEM((2, 3, rows, rows), jnp.float32),
            pltpu.VMEM((2, 3, rows, rows), jnp.float32),
            pltpu.VMEM((2, 3, rows, rows), jnp.float32),
            pltpu.VMEM((2, 3, rows, rows), jnp.bfloat16),
            pltpu.VMEM((2, 3, rows, rows), jnp.bfloat16),
            pltpu.VMEM((2, 2, rows, HEAD), jnp.float32),
            pltpu.SemaphoreType.DMA((6,)),
            pltpu.SemaphoreType.DMA((2, heads, 2)),
            pltpu.SemaphoreType.DMA((2, heads, 2)),
            pltpu.SemaphoreType.DMA((2, heads, 2)),
            pltpu.SemaphoreType.DMA((2, heads, 2)),
            pltpu.SemaphoreType.DMA((3, LINE)),
            pltpu.SemaphoreType.DMA((3, LINE)),
            pltpu.SemaphoreType.REGULAR((3,)),
        ],
        compiler_params=pltpu.CompilerParams(
            collective_id=0, has_side_effects=True, vmem_limit_bytes=40 * 1024 * 1024
        ),
        cost_estimate=pl.CostEstimate(
            flops=48 * heads * rows * rows * HEAD,
            bytes_accessed=8 * rows * width,
            transcendentals=4 * heads * rows * rows,
        ),
    )(*(pltpu.with_memory_space_constraint(array, pltpu.HBM) for array in inputs))
    return (*results, jnp.sum(total, axis=1))


def solution(mesh):
    return jax.shard_map(
        shards,
        mesh=mesh,
        in_specs=(
            P("rep", None),
            P("rep", "ctx", None),
            P("rep", "ctx"),
            P("rep", "ctx", None),
            P("rep", "ctx", None),
            P("rep", "ctx", None),
            P("rep", "ctx", None),
            P(),
        ),
        out_specs=(
            P("rep", "ctx", None),
            P("rep", "ctx", None),
            P("rep", "ctx", None),
            P("rep", "ctx", None),
            P(),
        ),
        check_vma=False,
    )
```

```python
import math

import jax
import jax.numpy as jnp
from jax import lax
from jax.experimental import pallas as pl
from jax.experimental.pallas import tpu as pltpu
from jax.sharding import PartitionSpec as P

WINDOW = 512
HEAD = 128
STRIP = 32
AHEAD = 3
LINE = 8
MESH = pl.DeviceIdType.MESH


def row_facts(offsets_ref, users, rows):
    start = jnp.zeros_like(rows)
    end = jnp.full_like(rows, 1 << 30)
    for user in range(users + 1):
        bound = offsets_ref[0, user]
        begun = rows >= bound
        start = jnp.where(begun, bound, start)
        end = jnp.where(begun, end, jnp.minimum(end, bound))
    length = jnp.minimum(end - start, WINDOW)
    return jnp.maximum(start, rows - (WINDOW - 1)), lax.rsqrt(length.astype(jnp.float32))


def fill_weights(offsets_ref, users, first, rows, weights):
    span = (rows, rows)
    down = lax.broadcasted_iota(jnp.int32, span, 0)
    across = lax.broadcasted_iota(jnp.int32, span, 1)
    lo, scale = row_facts(offsets_ref, users, first + lax.broadcasted_iota(jnp.int32, (rows, 1), 0))
    for segment, shift in ((0, 0), (1, -2 * rows), (2, -rows)):
        key = first + shift + across
        mask = (key >= lo) & (key <= first + down)
        weights[0, segment] = jnp.where(mask, scale, 0.0)
    for segment, shift in ((0, 0), (1, 2 * rows), (2, rows)):
        query = first + shift + lax.broadcasted_iota(jnp.int32, (1, rows), 1)
        lo, scale = row_facts(offsets_ref, users, query)
        key = first + down
        mask = (key >= lo) & (key <= query)
        weights[1, segment] = jnp.where(mask, scale, 0.0)


def dot_nt(left, right):
    return lax.dot_general(left, right, (((1,), (1,)), ((), ())), preferred_element_type=jnp.float32)


def dot_nn(left, right):
    return jnp.dot(left, right, preferred_element_type=jnp.float32)


def kernel(
    size,
    heads,
    users,
    offsets_hbm,
    alpha_hbm,
    q_hbm,
    k_hbm,
    v_hbm,
    g_hbm,
    out_ref,
    dq_ref,
    dk_ref,
    dv_ref,
    sum_ref,
    offsets_ref,
    alpha_ref,
    own,
    far,
    near,
    da_ref,
    share,
    gathered,
    weights,
    raw_s,
    gw_s,
    w_s,
    gr_s,
    acc,
    load_sem,
    fact_sem,
    far_send,
    far_recv,
    near_send,
    near_recv,
    share_send,
    share_recv,
    reached,
):
    rows = q_hbm.shape[1]
    coeff = 1.0 / math.sqrt(HEAD)
    me = lax.axis_index("ctx")
    core = lax.rem(me, 2)
    sibling = me + 1 - 2 * core
    ahead, behind = jnp.minimum(me + 2, size - 1), jnp.maximum(me - 2, 0)
    has_ahead, has_behind = me < size - 2, me >= 2
    arrays = (q_hbm, g_hbm, k_hbm, v_hbm)
    targets = (ahead, behind)
    sends, receives = (has_ahead, has_behind), (has_behind, has_ahead)
    direct = (core == 0, core == 1)
    relays = ((core == 1) & has_behind, (core == 0) & has_ahead)
    near_sends = (me != 1, me != size - 2)
    near_receives = (me != 0, me != size - 1)
    results = ((out_ref, dq_ref), (dv_ref, dk_ref))

    def head_of(step, d):
        return lax.rem(step + d * (heads // 2), heads)

    def columns(head):
        return pl.ds(pl.multiple_of(head * HEAD, HEAD), HEAD)

    def far_copy(step, d, m):
        head = head_of(step, d)
        return pltpu.make_async_remote_copy(
            src_ref=own.at[2 - 2 * d + m, :, columns(head)],
            dst_ref=far.at[d, head, m],
            send_sem=far_send.at[d, head, m],
            recv_sem=far_recv.at[d, head, m],
            device_id={"ctx": targets[d]},
            device_id_type=MESH,
        )

    def near_copy(step, d, m, forwarded):
        head = head_of(step, d)
        source = far.at[d, head, m] if forwarded else own.at[2 - 2 * d + m, :, columns(head)]
        return pltpu.make_async_remote_copy(
            src_ref=source,
            dst_ref=near.at[d, head, m],
            send_sem=near_send.at[d, head, m],
            recv_sem=near_recv.at[d, head, m],
            device_id={"ctx": sibling},
            device_id_type=MESH,
        )

    rep = lax.axis_index("rep")
    pair_x = rep * 2 + core
    y, z = lax.rem(me // 2, LINE), me // (2 * LINE)
    places = (pair_x, y, z)

    def member(stage, n):
        if stage == 0:
            return {"ctx": me - core + lax.rem(n, 2), "rep": n // 2}
        return {"ctx": me + (n - places[stage]) * (2 if stage == 1 else 2 * LINE), "rep": rep}

    def share_copy(stage, hop, slot):
        return pltpu.make_async_remote_copy(
            src_ref=share.at[stage],
            dst_ref=gathered.at[stage, slot],
            send_sem=share_send.at[stage, hop],
            recv_sem=share_recv.at[stage, slot],
            device_id=member(stage, lax.rem(places[stage] + hop, LINE)),
            device_id_type=MESH,
        )

    def share_start(stage, value):
        share[stage] = value
        gathered[stage, places[stage]] = value
        for hop in range(1, LINE):
            share_copy(stage, hop, places[stage]).start()

    def share_finish(stage):
        for hop in range(1, LINE):
            share_copy(stage, hop, lax.rem(places[stage] + hop, LINE)).wait_recv()
        return jnp.sum(gathered[stage], axis=0)

    def load(n, head):
        return pltpu.make_async_copy(
            arrays[n].at[0, :, columns(head)], own.at[n, :, columns(head)], load_sem.at[n, head]
        )

    def sent_at(step):
        return [(2 - 2 * d + m, head_of(step, d)) for d in range(2) for m in range(2)]

    facts = [
        pltpu.make_async_copy(offsets_hbm, offsets_ref, fact_sem.at[0]),
        pltpu.make_async_copy(alpha_hbm, alpha_ref, fact_sem.at[1]),
    ]

    @pl.loop(0, heads)
    def _(step):
        for piece in sent_at(step):
            load(*piece).start()

    for copy in facts:
        copy.start()
    def far_start(step):
        for d in range(2):

            @pl.when(sends[d])
            def _():
                for m in range(2):
                    far_copy(step, d, m).start()

    def near_start(step, conditions, forwarded):
        for d in range(2):

            @pl.when(conditions[d])
            def _():
                for m in range(2):
                    near_copy(step, d, m, forwarded).start()

    def wait_if(condition, *waits):
        @pl.when(condition)
        def _():
            for wait in waits:
                wait()

    barrier = pltpu.get_barrier_semaphore()

    def along_z(distance):
        inside = z + distance < LINE if distance > 0 else z + distance >= 0
        return inside, {"ctx": jnp.clip(me + 2 * LINE * distance, 0, size - 1)}

    def count(conditions):
        return sum(condition.astype(jnp.int32) for condition in conditions)

    greeted = [(has_ahead, {"ctx": ahead}), (has_behind, {"ctx": behind}), along_z(1), along_z(-1)]
    for exists, device in greeted:

        @pl.when(exists)
        def _():
            pl.semaphore_signal(barrier, inc=1, device_id=device, device_id_type=MESH)

    pl.semaphore_signal(barrier, inc=1, device_id={"ctx": sibling}, device_id_type=MESH)
    for stage in range(2):
        for hop in range(1, LINE):
            other = lax.rem(places[stage] + hop, LINE)
            pl.semaphore_signal(barrier, inc=1, device_id=member(stage, other), device_id_type=MESH)
    pl.semaphore_wait(barrier, 1 + 2 * (LINE - 1) + count([exists for exists, _ in greeted]))

    for step in range(AHEAD):
        for piece in sent_at(step):
            load(*piece).wait()
        far_start(step)
    for step in range(AHEAD):
        near_start(step, direct, False)

    def pass_on(n):
        for distance in (1 << n, -(1 << n)):
            exists, device = along_z(distance)

            @pl.when(exists)
            def _():
                pl.semaphore_signal(reached.at[n], inc=1, device_id=device, device_id_type=MESH)

    def learn(n):
        pl.semaphore_wait(reached.at[n], count([along_z(1 << n)[0], along_z(-(1 << n))[0]]))

    pass_on(0)
    for d in range(2):

        @pl.when(jnp.logical_not(receives[d]))
        def _():
            far[d] = jnp.zeros(far.shape[1:], far.dtype)

        @pl.when(jnp.logical_not(near_receives[d]))
        def _():
            near[d] = jnp.zeros(near.shape[1:], near.dtype)

    for copy in facts:
        copy.wait()
    fill_weights(offsets_ref, users, me * rows, rows, weights)
    lanes = lax.broadcasted_iota(jnp.int32, (STRIP, HEAD), 1)
    sublanes = lax.broadcasted_iota(jnp.int32, (STRIP, HEAD), 0)
    w_s[...] = jnp.zeros_like(w_s)
    gr_s[...] = jnp.zeros_like(gr_s)
    @pl.loop(AHEAD, heads)
    def _(step):
        for piece in sent_at(step):
            load(*piece).wait()

    def element(raw, gw, scale):
        half = raw * scale
        tanh = jnp.tanh(half)
        twice = 1.0 + tanh
        silu = half * twice
        return silu, gw * scale * (twice + silu * (1.0 - tanh))

    def weigh(d, segment, at, silu, grad):
        weight = weights[d, segment, *at]
        w_s[d, segment, *at] = (silu * weight).astype(jnp.bfloat16)
        scaled = grad * weight
        gr_s[d, segment, *at] = scaled.astype(jnp.bfloat16)
        return scaled

    def fold(product):
        return jnp.sum(product.reshape(-1, 8, HEAD), axis=0)

    def own_rows(n, head):
        return own[n, :, columns(head)]

    middle = heads // 2 - 1

    @pl.loop(0, heads)
    def _(step):
        for d in range(2):
            wait_if(receives[d], *(far_copy(step, d, m).wait_recv for m in range(2)))
        near_start(step, relays, True)

        @pl.when(step + AHEAD < heads)
        def _():
            for d in range(2):
                wait_if(sends[d], *(far_copy(step, d, m).wait_send for m in range(2)))
            far_start(step + AHEAD)
            near_start(step + AHEAD, direct, False)

        for n in range(2):

            @pl.when(step == 2 * n + 2)
            def _():
                learn(n)
                pass_on(n + 1)

        for stage in range(1, 3):

            @pl.when(step == middle + 1 + stage)
            def _():
                if stage == 2:
                    learn(2)
                share_start(stage, share_finish(stage - 1))

        for d in range(2):
            head = head_of(step, d)
            r1, r2 = own_rows(2 * d, head), own_rows(2 * d + 1, head)
            raw_s[d, 0] = dot_nt(r1, own_rows(2 - 2 * d, head))
            raw_s[d, 1] = dot_nt(r1, far[d, head, 0])
            gw_s[d, 0] = dot_nt(r2, own_rows(3 - 2 * d, head))
            gw_s[d, 1] = dot_nt(r2, far[d, head, 1])
        for d in range(2):
            head = head_of(step, d)
            scale = 0.5 * coeff * alpha_ref[head]
            total = jnp.zeros((8, HEAD), jnp.float32)
            for row in range(0, rows, STRIP):
                for column in range(0, rows, HEAD):
                    at = (pl.ds(row, STRIP), pl.ds(column, HEAD))
                    if row // HEAD == column // HEAD:
                        gap = column - row + lanes - sublanes
                        mine = gap <= 0 if d == 0 else gap >= 0
                        raw = jnp.where(mine, raw_s[d, 0, *at], raw_s[d, 1, *at])
                        gw = jnp.where(mine, gw_s[d, 0, *at], gw_s[d, 1, *at])
                        silu, grad = element(raw, gw, scale)
                        total += fold((weigh(d, 0, at, silu, grad) + weigh(d, 1, at, silu, grad)) * raw)
                    else:
                        segment = int((row < column) == (d == 0))
                        raw = raw_s[d, segment, *at]
                        silu, grad = element(raw, gw_s[d, segment, *at], scale)
                        total += fold(weigh(d, segment, at, silu, grad) * raw)
            da_ref[d, step] = total / alpha_ref[head]
            acc[d, 0] = dot_nn(w_s[d, 0], own_rows(3 - 2 * d, head)) + dot_nn(w_s[d, 1], far[d, head, 1])
            acc[d, 1] = dot_nn(gr_s[d, 0], own_rows(2 - 2 * d, head)) + dot_nn(gr_s[d, 1], far[d, head, 0])

        for d in range(2):
            wait_if(near_receives[d], *(near_copy(step, d, m, True).wait_recv for m in range(2)))
        for d in range(2):
            head = head_of(step, d)
            raw_s[d, 2] = dot_nt(own_rows(2 * d, head), near[d, head, 0])
            gw_s[d, 2] = dot_nt(own_rows(2 * d + 1, head), near[d, head, 1])
        for d in range(2):
            head = head_of(step, d)
            scale = 0.5 * coeff * alpha_ref[head]
            total = jnp.zeros((8, HEAD), jnp.float32)
            for row in range(0, rows, STRIP):
                for column in range(0, rows, HEAD):
                    at = (pl.ds(row, STRIP), pl.ds(column, HEAD))
                    raw = raw_s[d, 2, *at]
                    silu, grad = element(raw, gw_s[d, 2, *at], scale)
                    total += fold(weigh(d, 2, at, silu, grad) * raw)
            da_ref[d, step] += total / alpha_ref[head]
            first = acc[d, 0] + dot_nn(w_s[d, 2], near[d, head, 1])
            second = acc[d, 1] + dot_nn(gr_s[d, 2], near[d, head, 0])
            results[d][0][0, :, columns(head)] = first.astype(jnp.bfloat16)
            results[d][1][0, :, columns(head)] = second.astype(jnp.bfloat16)

        @pl.when(step == middle)
        def _():
            for d in range(2):
                half = pl.ds(d * (heads // 2), heads // 2)
                share[0, half] = jnp.sum(da_ref[d, pl.ds(0, heads // 2)], axis=1)
            share_start(0, share[0])

    @pl.loop(0, heads)
    def _(step):
        for d in range(2):
            wait_if(
                sends[d] & (step + AHEAD >= heads), *(far_copy(step, d, m).wait_send for m in range(2))
            )
            wait_if(near_sends[d], *(near_copy(step, d, m, True).wait_send for m in range(2)))

    sum_ref[...] = share_finish(2)
    for stage in range(3):
        for hop in range(1, LINE):
            share_copy(stage, hop, places[stage]).wait_send()


def shards(offsets, pairs, pair_count, queries, keys, values, cotangent, alpha):
    rows, width = queries.shape[1:]
    heads = alpha.shape[0]
    size = lax.axis_size("ctx")
    anywhere = pl.BlockSpec(memory_space=pl.ANY)

    def body(*refs):
        kernel(size, heads, offsets.shape[1] - 1, *refs)

    inputs = (offsets, alpha, queries, keys, values, cotangent)
    in_vmem = pltpu.VMEM((1, rows, width), jnp.bfloat16)
    *results, total = pl.pallas_call(
        body,
        out_shape=(in_vmem,) * 4 + (pltpu.VMEM((heads, HEAD), jnp.float32),),
        in_specs=[anywhere] * 6,
        out_specs=[pl.BlockSpec(memory_space=pltpu.VMEM)] * 5,
        scratch_shapes=[
            pltpu.SMEM(offsets.shape, jnp.int32),
            pltpu.SMEM(alpha.shape, jnp.float32),
            pltpu.VMEM((4, rows, width), jnp.bfloat16),
            pltpu.VMEM((2, heads, 2, rows, HEAD), jnp.bfloat16),
            pltpu.VMEM((2, heads, 2, rows, HEAD), jnp.bfloat16),
            pltpu.VMEM((2, heads, 8, HEAD), jnp.float32),
            pltpu.VMEM((3, heads, HEAD), jnp.float32),
            pltpu.VMEM((3, LINE, heads, HEAD), jnp.float32),
            pltpu.VMEM((2, 3, rows, rows), jnp.float32),
            pltpu.VMEM((2, 3, rows, rows), jnp.float32),
            pltpu.VMEM((2, 3, rows, rows), jnp.float32),
            pltpu.VMEM((2, 3, rows, rows), jnp.bfloat16),
            pltpu.VMEM((2, 3, rows, rows), jnp.bfloat16),
            pltpu.VMEM((2, 2, rows, HEAD), jnp.float32),
            pltpu.SemaphoreType.DMA((4, heads)),
            pltpu.SemaphoreType.DMA((2,)),
            pltpu.SemaphoreType.DMA((2, heads, 2)),
            pltpu.SemaphoreType.DMA((2, heads, 2)),
            pltpu.SemaphoreType.DMA((2, heads, 2)),
            pltpu.SemaphoreType.DMA((2, heads, 2)),
            pltpu.SemaphoreType.DMA((3, LINE)),
            pltpu.SemaphoreType.DMA((3, LINE)),
            pltpu.SemaphoreType.REGULAR((3,)),
        ],
        compiler_params=pltpu.CompilerParams(
            collective_id=0, has_side_effects=True, vmem_limit_bytes=40 * 1024 * 1024
        ),
        cost_estimate=pl.CostEstimate(
            flops=48 * heads * rows * rows * HEAD,
            bytes_accessed=8 * rows * width,
            transcendentals=4 * heads * rows * rows,
        ),
    )(*(pltpu.with_memory_space_constraint(array, pltpu.HBM) for array in inputs))
    return (*results, jnp.sum(total, axis=1))


def solution(mesh):
    return jax.shard_map(
        shards,
        mesh=mesh,
        in_specs=(
            P("rep", None),
            P("rep", "ctx", None),
            P("rep", "ctx"),
            P("rep", "ctx", None),
            P("rep", "ctx", None),
            P("rep", "ctx", None),
            P("rep", "ctx", None),
            P(),
        ),
        out_specs=(
            P("rep", "ctx", None),
            P("rep", "ctx", None),
            P("rep", "ctx", None),
            P("rep", "ctx", None),
            P(),
        ),
        check_vma=False,
    )
```

```python
import math

import jax
import jax.numpy as jnp
from jax import lax
from jax.experimental import pallas as pl
from jax.experimental.pallas import tpu as pltpu
from jax.sharding import PartitionSpec as P

WINDOW = 512
HEAD = 128
STRIP = 32
AHEAD = 2
LINE = 8
MESH = pl.DeviceIdType.MESH


def row_facts(offsets_ref, users, rows):
    start = jnp.zeros_like(rows)
    end = jnp.full_like(rows, 1 << 30)
    for user in range(users + 1):
        bound = offsets_ref[0, user]
        begun = rows >= bound
        start = jnp.where(begun, bound, start)
        end = jnp.where(begun, end, jnp.minimum(end, bound))
    length = jnp.minimum(end - start, WINDOW)
    return jnp.maximum(start, rows - (WINDOW - 1)), lax.rsqrt(length.astype(jnp.float32))


def fill_weights(offsets_ref, users, first, rows, weights):
    span = (rows, rows)
    down = lax.broadcasted_iota(jnp.int32, span, 0)
    across = lax.broadcasted_iota(jnp.int32, span, 1)
    lo, scale = row_facts(offsets_ref, users, first + lax.broadcasted_iota(jnp.int32, (rows, 1), 0))
    for segment, shift in ((0, 0), (1, -2 * rows), (2, -rows)):
        key = first + shift + across
        mask = (key >= lo) & (key <= first + down)
        weights[0, segment] = jnp.where(mask, scale, 0.0)
    for segment, shift in ((0, 0), (1, 2 * rows), (2, rows)):
        query = first + shift + lax.broadcasted_iota(jnp.int32, (1, rows), 1)
        lo, scale = row_facts(offsets_ref, users, query)
        key = first + down
        mask = (key >= lo) & (key <= query)
        weights[1, segment] = jnp.where(mask, scale, 0.0)


def dot_nt(left, right):
    return lax.dot_general(left, right, (((1,), (1,)), ((), ())), preferred_element_type=jnp.float32)


def dot_nn(left, right):
    return jnp.dot(left, right, preferred_element_type=jnp.float32)


def kernel(
    size,
    heads,
    users,
    offsets_hbm,
    alpha_hbm,
    q_hbm,
    k_hbm,
    v_hbm,
    g_hbm,
    out_ref,
    dq_ref,
    dk_ref,
    dv_ref,
    sum_ref,
    offsets_ref,
    alpha_ref,
    own,
    far,
    near,
    da_ref,
    share,
    gathered,
    weights,
    raw_s,
    gw_s,
    w_s,
    gr_s,
    acc,
    load_sem,
    fact_sem,
    far_send,
    far_recv,
    near_send,
    near_recv,
    share_send,
    share_recv,
    reached,
):
    rows = q_hbm.shape[1]
    coeff = 1.0 / math.sqrt(HEAD)
    me = lax.axis_index("ctx")
    core = lax.rem(me, 2)
    sibling = me + 1 - 2 * core
    ahead, behind = jnp.minimum(me + 2, size - 1), jnp.maximum(me - 2, 0)
    has_ahead, has_behind = me < size - 2, me >= 2
    arrays = (q_hbm, g_hbm, k_hbm, v_hbm)
    targets = (ahead, behind)
    sends, receives = (has_ahead, has_behind), (has_behind, has_ahead)
    direct = (core == 0, core == 1)
    relays = ((core == 1) & has_behind, (core == 0) & has_ahead)
    near_sends = (me != 1, me != size - 2)
    near_receives = (me != 0, me != size - 1)
    results = ((out_ref, dq_ref), (dv_ref, dk_ref))

    def head_of(step, d):
        return lax.rem(step + d * (heads // 2), heads)

    def columns(head):
        return pl.ds(pl.multiple_of(head * HEAD, HEAD), HEAD)

    def far_copy(step, d, m):
        head = head_of(step, d)
        return pltpu.make_async_remote_copy(
            src_ref=own.at[2 - 2 * d + m, :, columns(head)],
            dst_ref=far.at[d, head, m],
            send_sem=far_send.at[d, head, m],
            recv_sem=far_recv.at[d, head, m],
            device_id={"ctx": targets[d]},
            device_id_type=MESH,
        )

    def near_copy(step, d, m, forwarded):
        head = head_of(step, d)
        source = far.at[d, head, m] if forwarded else own.at[2 - 2 * d + m, :, columns(head)]
        return pltpu.make_async_remote_copy(
            src_ref=source,
            dst_ref=near.at[d, head, m],
            send_sem=near_send.at[d, head, m],
            recv_sem=near_recv.at[d, head, m],
            device_id={"ctx": sibling},
            device_id_type=MESH,
        )

    rep = lax.axis_index("rep")
    pair_x = rep * 2 + core
    y, z = lax.rem(me // 2, LINE), me // (2 * LINE)
    places = (pair_x, y, z)

    def member(stage, n):
        if stage == 0:
            return {"ctx": me - core + lax.rem(n, 2), "rep": n // 2}
        return {"ctx": me + (n - places[stage]) * (2 if stage == 1 else 2 * LINE), "rep": rep}

    def share_copy(stage, hop, slot):
        return pltpu.make_async_remote_copy(
            src_ref=share.at[stage],
            dst_ref=gathered.at[stage, slot],
            send_sem=share_send.at[stage, hop],
            recv_sem=share_recv.at[stage, slot],
            device_id=member(stage, lax.rem(places[stage] + hop, LINE)),
            device_id_type=MESH,
        )

    def share_start(stage, value):
        share[stage] = value
        gathered[stage, places[stage]] = value
        for hop in range(1, LINE):
            share_copy(stage, hop, places[stage]).start()

    def share_finish(stage):
        for hop in range(1, LINE):
            share_copy(stage, hop, lax.rem(places[stage] + hop, LINE)).wait_recv()
        return jnp.sum(gathered[stage], axis=0)

    def load(n, head):
        return pltpu.make_async_copy(
            arrays[n].at[0, :, columns(head)], own.at[n, :, columns(head)], load_sem.at[n, head]
        )

    def sent_at(step):
        return [(2 - 2 * d + m, head_of(step, d)) for d in range(2) for m in range(2)]

    facts = [
        pltpu.make_async_copy(offsets_hbm, offsets_ref, fact_sem.at[0]),
        pltpu.make_async_copy(alpha_hbm, alpha_ref, fact_sem.at[1]),
    ]

    @pl.loop(0, heads)
    def _(step):
        for piece in sent_at(step):
            load(*piece).start()

    for copy in facts:
        copy.start()
    def far_start(step):
        for d in range(2):

            @pl.when(sends[d])
            def _():
                for m in range(2):
                    far_copy(step, d, m).start()

    def near_start(step, conditions, forwarded):
        for d in range(2):

            @pl.when(conditions[d])
            def _():
                for m in range(2):
                    near_copy(step, d, m, forwarded).start()

    def wait_if(condition, *waits):
        @pl.when(condition)
        def _():
            for wait in waits:
                wait()

    barrier = pltpu.get_barrier_semaphore()

    def along_z(distance):
        inside = z + distance < LINE if distance > 0 else z + distance >= 0
        return inside, {"ctx": jnp.clip(me + 2 * LINE * distance, 0, size - 1)}

    def count(conditions):
        return sum(condition.astype(jnp.int32) for condition in conditions)

    greeted = [(has_ahead, {"ctx": ahead}), (has_behind, {"ctx": behind}), along_z(1), along_z(-1)]
    for exists, device in greeted:

        @pl.when(exists)
        def _():
            pl.semaphore_signal(barrier, inc=1, device_id=device, device_id_type=MESH)

    pl.semaphore_signal(barrier, inc=1, device_id={"ctx": sibling}, device_id_type=MESH)
    for stage in range(2):
        for hop in range(1, LINE):
            other = lax.rem(places[stage] + hop, LINE)
            pl.semaphore_signal(barrier, inc=1, device_id=member(stage, other), device_id_type=MESH)
    pl.semaphore_wait(barrier, 1 + 2 * (LINE - 1) + count([exists for exists, _ in greeted]))

    for step in range(AHEAD):
        for piece in sent_at(step):
            load(*piece).wait()
        far_start(step)
    for step in range(AHEAD):
        near_start(step, direct, False)

    def pass_on(n):
        for distance in (1 << n, -(1 << n)):
            exists, device = along_z(distance)

            @pl.when(exists)
            def _():
                pl.semaphore_signal(reached.at[n], inc=1, device_id=device, device_id_type=MESH)

    def learn(n):
        pl.semaphore_wait(reached.at[n], count([along_z(1 << n)[0], along_z(-(1 << n))[0]]))

    pass_on(0)
    for d in range(2):

        @pl.when(jnp.logical_not(receives[d]))
        def _():
            far[d] = jnp.zeros(far.shape[1:], far.dtype)

        @pl.when(jnp.logical_not(near_receives[d]))
        def _():
            near[d] = jnp.zeros(near.shape[1:], near.dtype)

    for copy in facts:
        copy.wait()
    fill_weights(offsets_ref, users, me * rows, rows, weights)
    lanes = lax.broadcasted_iota(jnp.int32, (STRIP, HEAD), 1)
    sublanes = lax.broadcasted_iota(jnp.int32, (STRIP, HEAD), 0)
    w_s[...] = jnp.zeros_like(w_s)
    gr_s[...] = jnp.zeros_like(gr_s)
    @pl.loop(AHEAD, heads)
    def _(step):
        for piece in sent_at(step):
            load(*piece).wait()

    def element(raw, gw, scale):
        half = raw * scale
        tanh = jnp.tanh(half)
        twice = 1.0 + tanh
        silu = half * twice
        return silu, gw * scale * (twice + silu * (1.0 - tanh))

    def weigh(d, segment, at, silu, grad):
        weight = weights[d, segment, *at]
        w_s[d, segment, *at] = (silu * weight).astype(jnp.bfloat16)
        scaled = grad * weight
        gr_s[d, segment, *at] = scaled.astype(jnp.bfloat16)
        return scaled

    def fold(product):
        return jnp.sum(product.reshape(-1, 8, HEAD), axis=0)

    def own_rows(n, head):
        return own[n, :, columns(head)]

    middle = heads // 2 - 1

    def send_next(step):
        for d in range(2):
            wait_if(sends[d], *(far_copy(step, d, m).wait_send for m in range(2)))
        far_start(step + AHEAD)
        near_start(step + AHEAD, direct, False)

    @pl.loop(0, heads)
    def _(step):
        for d in range(2):
            wait_if(receives[d], *(far_copy(step, d, m).wait_recv for m in range(2)))
        near_start(step, relays, True)

        @pl.when(step < middle)
        def _():
            send_next(step)

        for n in range(2):

            @pl.when(step == 2 * n + 2)
            def _():
                learn(n)
                pass_on(n + 1)

        for d in range(2):
            head = head_of(step, d)
            r1, r2 = own_rows(2 * d, head), own_rows(2 * d + 1, head)
            raw_s[d, 0] = dot_nt(r1, own_rows(2 - 2 * d, head))
            raw_s[d, 1] = dot_nt(r1, far[d, head, 0])
            gw_s[d, 0] = dot_nt(r2, own_rows(3 - 2 * d, head))
            gw_s[d, 1] = dot_nt(r2, far[d, head, 1])
        for d in range(2):
            head = head_of(step, d)
            scale = 0.5 * coeff * alpha_ref[head]
            total = jnp.zeros((8, HEAD), jnp.float32)
            for row in range(0, rows, STRIP):
                for column in range(0, rows, HEAD):
                    at = (pl.ds(row, STRIP), pl.ds(column, HEAD))
                    if row // HEAD == column // HEAD:
                        gap = column - row + lanes - sublanes
                        mine = gap <= 0 if d == 0 else gap >= 0
                        raw = jnp.where(mine, raw_s[d, 0, *at], raw_s[d, 1, *at])
                        gw = jnp.where(mine, gw_s[d, 0, *at], gw_s[d, 1, *at])
                        silu, grad = element(raw, gw, scale)
                        total += fold((weigh(d, 0, at, silu, grad) + weigh(d, 1, at, silu, grad)) * raw)
                    else:
                        segment = int((row < column) == (d == 0))
                        raw = raw_s[d, segment, *at]
                        silu, grad = element(raw, gw_s[d, segment, *at], scale)
                        total += fold(weigh(d, segment, at, silu, grad) * raw)
            da_ref[d, step] = total / alpha_ref[head]
            acc[d, 0] = dot_nn(w_s[d, 0], own_rows(3 - 2 * d, head)) + dot_nn(w_s[d, 1], far[d, head, 1])
            acc[d, 1] = dot_nn(gr_s[d, 0], own_rows(2 - 2 * d, head)) + dot_nn(gr_s[d, 1], far[d, head, 0])

        for stage in range(1, 3):

            @pl.when(step == middle + stage)
            def _():
                if stage == 2:
                    learn(2)
                share_start(stage, share_finish(stage - 1))
                send_next(step)

        for d in range(2):
            wait_if(near_receives[d], *(near_copy(step, d, m, True).wait_recv for m in range(2)))
        for d in range(2):
            head = head_of(step, d)
            raw_s[d, 2] = dot_nt(own_rows(2 * d, head), near[d, head, 0])
            gw_s[d, 2] = dot_nt(own_rows(2 * d + 1, head), near[d, head, 1])
        for d in range(2):
            head = head_of(step, d)
            scale = 0.5 * coeff * alpha_ref[head]
            total = jnp.zeros((8, HEAD), jnp.float32)
            for row in range(0, rows, STRIP):
                for column in range(0, rows, HEAD):
                    at = (pl.ds(row, STRIP), pl.ds(column, HEAD))
                    raw = raw_s[d, 2, *at]
                    silu, grad = element(raw, gw_s[d, 2, *at], scale)
                    total += fold(weigh(d, 2, at, silu, grad) * raw)
            da_ref[d, step] += total / alpha_ref[head]
            first = acc[d, 0] + dot_nn(w_s[d, 2], near[d, head, 1])
            second = acc[d, 1] + dot_nn(gr_s[d, 2], near[d, head, 0])
            results[d][0][0, :, columns(head)] = first.astype(jnp.bfloat16)
            results[d][1][0, :, columns(head)] = second.astype(jnp.bfloat16)

        @pl.when(step == middle)
        def _():
            for d in range(2):
                half = pl.ds(d * (heads // 2), heads // 2)
                share[0, half] = jnp.sum(da_ref[d, pl.ds(0, heads // 2)], axis=1)
            share_start(0, share[0])
            send_next(step)

    @pl.loop(0, heads)
    def _(step):
        for d in range(2):
            wait_if(
                sends[d] & (step + AHEAD >= heads), *(far_copy(step, d, m).wait_send for m in range(2))
            )
            wait_if(near_sends[d], *(near_copy(step, d, m, True).wait_send for m in range(2)))

    sum_ref[...] = share_finish(2)
    for stage in range(3):
        for hop in range(1, LINE):
            share_copy(stage, hop, places[stage]).wait_send()


def shards(offsets, pairs, pair_count, queries, keys, values, cotangent, alpha):
    rows, width = queries.shape[1:]
    heads = alpha.shape[0]
    size = lax.axis_size("ctx")
    anywhere = pl.BlockSpec(memory_space=pl.ANY)

    def body(*refs):
        kernel(size, heads, offsets.shape[1] - 1, *refs)

    inputs = (offsets, alpha, queries, keys, values, cotangent)
    in_vmem = pltpu.VMEM((1, rows, width), jnp.bfloat16)
    *results, total = pl.pallas_call(
        body,
        out_shape=(in_vmem,) * 4 + (pltpu.VMEM((heads, HEAD), jnp.float32),),
        in_specs=[anywhere] * 6,
        out_specs=[pl.BlockSpec(memory_space=pltpu.VMEM)] * 5,
        scratch_shapes=[
            pltpu.SMEM(offsets.shape, jnp.int32),
            pltpu.SMEM(alpha.shape, jnp.float32),
            pltpu.VMEM((4, rows, width), jnp.bfloat16),
            pltpu.VMEM((2, heads, 2, rows, HEAD), jnp.bfloat16),
            pltpu.VMEM((2, heads, 2, rows, HEAD), jnp.bfloat16),
            pltpu.VMEM((2, heads, 8, HEAD), jnp.float32),
            pltpu.VMEM((3, heads, HEAD), jnp.float32),
            pltpu.VMEM((3, LINE, heads, HEAD), jnp.float32),
            pltpu.VMEM((2, 3, rows, rows), jnp.float32),
            pltpu.VMEM((2, 3, rows, rows), jnp.float32),
            pltpu.VMEM((2, 3, rows, rows), jnp.float32),
            pltpu.VMEM((2, 3, rows, rows), jnp.bfloat16),
            pltpu.VMEM((2, 3, rows, rows), jnp.bfloat16),
            pltpu.VMEM((2, 2, rows, HEAD), jnp.float32),
            pltpu.SemaphoreType.DMA((4, heads)),
            pltpu.SemaphoreType.DMA((2,)),
            pltpu.SemaphoreType.DMA((2, heads, 2)),
            pltpu.SemaphoreType.DMA((2, heads, 2)),
            pltpu.SemaphoreType.DMA((2, heads, 2)),
            pltpu.SemaphoreType.DMA((2, heads, 2)),
            pltpu.SemaphoreType.DMA((3, LINE)),
            pltpu.SemaphoreType.DMA((3, LINE)),
            pltpu.SemaphoreType.REGULAR((3,)),
        ],
        compiler_params=pltpu.CompilerParams(
            collective_id=0, has_side_effects=True, vmem_limit_bytes=40 * 1024 * 1024
        ),
        cost_estimate=pl.CostEstimate(
            flops=48 * heads * rows * rows * HEAD,
            bytes_accessed=8 * rows * width,
            transcendentals=4 * heads * rows * rows,
        ),
    )(*(pltpu.with_memory_space_constraint(array, pltpu.HBM) for array in inputs))
    return (*results, jnp.sum(total, axis=1))


def solution(mesh):
    return jax.shard_map(
        shards,
        mesh=mesh,
        in_specs=(
            P("rep", None),
            P("rep", "ctx", None),
            P("rep", "ctx"),
            P("rep", "ctx", None),
            P("rep", "ctx", None),
            P("rep", "ctx", None),
            P("rep", "ctx", None),
            P(),
        ),
        out_specs=(
            P("rep", "ctx", None),
            P("rep", "ctx", None),
            P("rep", "ctx", None),
            P("rep", "ctx", None),
            P(),
        ),
        check_vma=False,
    )
```

```python
import math

import jax
import jax.numpy as jnp
from jax import lax
from jax.experimental import pallas as pl
from jax.experimental.pallas import tpu as pltpu
from jax.sharding import PartitionSpec as P

WINDOW = 512
HEAD = 128
STRIP = 32
AHEAD = 3
LINE = 8
MESH = pl.DeviceIdType.MESH


def row_facts(offsets_ref, users, rows):
    start = jnp.zeros_like(rows)
    end = jnp.full_like(rows, 1 << 30)
    for user in range(users + 1):
        bound = offsets_ref[0, user]
        begun = rows >= bound
        start = jnp.where(begun, bound, start)
        end = jnp.where(begun, end, jnp.minimum(end, bound))
    length = jnp.minimum(end - start, WINDOW)
    return jnp.maximum(start, rows - (WINDOW - 1)), lax.rsqrt(length.astype(jnp.float32))


def fill_weights(offsets_ref, users, first, rows, weights):
    span = (rows, rows)
    down = lax.broadcasted_iota(jnp.int32, span, 0)
    across = lax.broadcasted_iota(jnp.int32, span, 1)
    lo, scale = row_facts(offsets_ref, users, first + lax.broadcasted_iota(jnp.int32, (rows, 1), 0))
    for segment, shift in ((0, 0), (1, -2 * rows), (2, -rows)):
        key = first + shift + across
        mask = (key >= lo) & (key <= first + down)
        weights[0, segment] = jnp.where(mask, scale, 0.0)
    for segment, shift in ((0, 0), (1, 2 * rows), (2, rows)):
        query = first + shift + lax.broadcasted_iota(jnp.int32, (1, rows), 1)
        lo, scale = row_facts(offsets_ref, users, query)
        key = first + down
        mask = (key >= lo) & (key <= query)
        weights[1, segment] = jnp.where(mask, scale, 0.0)


def dot_nt(left, right):
    return lax.dot_general(left, right, (((1,), (1,)), ((), ())), preferred_element_type=jnp.float32)


def dot_nn(left, right):
    return jnp.dot(left, right, preferred_element_type=jnp.float32)


def kernel(
    size,
    heads,
    users,
    offsets_hbm,
    alpha_hbm,
    q_hbm,
    k_hbm,
    v_hbm,
    g_hbm,
    out_ref,
    dq_ref,
    dk_ref,
    dv_ref,
    sum_ref,
    offsets_ref,
    alpha_ref,
    own,
    far,
    near,
    da_ref,
    share,
    gathered,
    weights,
    raw_s,
    gw_s,
    w_s,
    gr_s,
    acc,
    load_sem,
    fact_sem,
    far_send,
    far_recv,
    near_send,
    near_recv,
    share_send,
    share_recv,
    reached,
):
    rows = q_hbm.shape[1]
    coeff = 1.0 / math.sqrt(HEAD)
    me = lax.axis_index("ctx")
    core = lax.rem(me, 2)
    sibling = me + 1 - 2 * core
    ahead, behind = jnp.minimum(me + 2, size - 1), jnp.maximum(me - 2, 0)
    has_ahead, has_behind = me < size - 2, me >= 2
    arrays = (q_hbm, g_hbm, k_hbm, v_hbm)
    targets = (ahead, behind)
    sends, receives = (has_ahead, has_behind), (has_behind, has_ahead)
    direct = (core == 0, core == 1)
    relays = ((core == 1) & has_behind, (core == 0) & has_ahead)
    near_sends = (me != 1, me != size - 2)
    near_receives = (me != 0, me != size - 1)
    results = ((out_ref, dq_ref), (dv_ref, dk_ref))

    def head_of(step, d):
        return lax.rem(step + d * (heads // 2), heads)

    def columns(head):
        return pl.ds(pl.multiple_of(head * HEAD, HEAD), HEAD)

    def far_copy(step, d, m):
        head = head_of(step, d)
        return pltpu.make_async_remote_copy(
            src_ref=own.at[2 - 2 * d + m, :, columns(head)],
            dst_ref=far.at[d, head, m],
            send_sem=far_send.at[d, head, m],
            recv_sem=far_recv.at[d, head, m],
            device_id={"ctx": targets[d]},
            device_id_type=MESH,
        )

    def near_copy(step, d, m, forwarded):
        head = head_of(step, d)
        source = far.at[d, head, m] if forwarded else own.at[2 - 2 * d + m, :, columns(head)]
        return pltpu.make_async_remote_copy(
            src_ref=source,
            dst_ref=near.at[d, head, m],
            send_sem=near_send.at[d, head, m],
            recv_sem=near_recv.at[d, head, m],
            device_id={"ctx": sibling},
            device_id_type=MESH,
        )

    rep = lax.axis_index("rep")
    pair_x = rep * 2 + core
    y, z = lax.rem(me // 2, LINE), me // (2 * LINE)
    places = (pair_x, y, z)

    def member(stage, n):
        if stage == 0:
            return {"ctx": me - core + lax.rem(n, 2), "rep": n // 2}
        return {"ctx": me + (n - places[stage]) * (2 if stage == 1 else 2 * LINE), "rep": rep}

    def share_copy(stage, hop, slot):
        return pltpu.make_async_remote_copy(
            src_ref=share.at[stage],
            dst_ref=gathered.at[stage, slot],
            send_sem=share_send.at[stage, hop],
            recv_sem=share_recv.at[stage, slot],
            device_id=member(stage, lax.rem(places[stage] + hop, LINE)),
            device_id_type=MESH,
        )

    def share_start(stage, value):
        share[stage] = value
        gathered[stage, places[stage]] = value
        for hop in range(1, LINE):
            share_copy(stage, hop, places[stage]).start()

    def share_finish(stage):
        for hop in range(1, LINE):
            share_copy(stage, hop, lax.rem(places[stage] + hop, LINE)).wait_recv()
        return jnp.sum(gathered[stage], axis=0)

    def load(n, head):
        return pltpu.make_async_copy(
            arrays[n].at[0, :, columns(head)], own.at[n, :, columns(head)], load_sem.at[n, head]
        )

    def sent_at(step):
        return [(2 - 2 * d + m, head_of(step, d)) for d in range(2) for m in range(2)]

    facts = [
        pltpu.make_async_copy(offsets_hbm, offsets_ref, fact_sem.at[0]),
        pltpu.make_async_copy(alpha_hbm, alpha_ref, fact_sem.at[1]),
    ]

    @pl.loop(0, heads)
    def _(step):
        for piece in sent_at(step):
            load(*piece).start()

    for copy in facts:
        copy.start()
    def far_start(step):
        for first in range(2):
            for m in range(2):
                for d in (first, 1 - first):

                    @pl.when((core == first) & sends[d])
                    def _():
                        far_copy(step, d, m).start()

    def near_start(step, conditions, forwarded):
        for d in range(2):

            @pl.when(conditions[d])
            def _():
                for m in range(2):
                    near_copy(step, d, m, forwarded).start()

    def wait_if(condition, *waits):
        @pl.when(condition)
        def _():
            for wait in waits:
                wait()

    barrier = pltpu.get_barrier_semaphore()

    def along_z(distance):
        inside = z + distance < LINE if distance > 0 else z + distance >= 0
        return inside, {"ctx": jnp.clip(me + 2 * LINE * distance, 0, size - 1)}

    def count(conditions):
        return sum(condition.astype(jnp.int32) for condition in conditions)

    greeted = [(has_ahead, {"ctx": ahead}), (has_behind, {"ctx": behind}), along_z(1), along_z(-1)]
    for exists, device in greeted:

        @pl.when(exists)
        def _():
            pl.semaphore_signal(barrier, inc=1, device_id=device, device_id_type=MESH)

    pl.semaphore_signal(barrier, inc=1, device_id={"ctx": sibling}, device_id_type=MESH)
    for stage in range(2):
        for hop in range(1, LINE):
            other = lax.rem(places[stage] + hop, LINE)
            pl.semaphore_signal(barrier, inc=1, device_id=member(stage, other), device_id_type=MESH)
    pl.semaphore_wait(barrier, 1 + 2 * (LINE - 1) + count([exists for exists, _ in greeted]))

    for step in range(AHEAD):
        for piece in sent_at(step):
            load(*piece).wait()
        far_start(step)
    for step in range(AHEAD):
        near_start(step, direct, False)

    def pass_on(n):
        for distance in (1 << n, -(1 << n)):
            exists, device = along_z(distance)

            @pl.when(exists)
            def _():
                pl.semaphore_signal(reached.at[n], inc=1, device_id=device, device_id_type=MESH)

    def learn(n):
        pl.semaphore_wait(reached.at[n], count([along_z(1 << n)[0], along_z(-(1 << n))[0]]))

    pass_on(0)
    for d in range(2):

        @pl.when(jnp.logical_not(receives[d]))
        def _():
            far[d] = jnp.zeros(far.shape[1:], far.dtype)

        @pl.when(jnp.logical_not(near_receives[d]))
        def _():
            near[d] = jnp.zeros(near.shape[1:], near.dtype)

    for copy in facts:
        copy.wait()
    fill_weights(offsets_ref, users, me * rows, rows, weights)
    lanes = lax.broadcasted_iota(jnp.int32, (STRIP, HEAD), 1)
    sublanes = lax.broadcasted_iota(jnp.int32, (STRIP, HEAD), 0)
    w_s[...] = jnp.zeros_like(w_s)
    gr_s[...] = jnp.zeros_like(gr_s)
    @pl.loop(AHEAD, heads)
    def _(step):
        for piece in sent_at(step):
            load(*piece).wait()

    def element(raw, gw, scale):
        half = raw * scale
        tanh = jnp.tanh(half)
        twice = 1.0 + tanh
        silu = half * twice
        return silu, gw * scale * (twice + silu * (1.0 - tanh))

    def weigh(d, segment, at, silu, grad):
        weight = weights[d, segment, *at]
        w_s[d, segment, *at] = (silu * weight).astype(jnp.bfloat16)
        scaled = grad * weight
        gr_s[d, segment, *at] = scaled.astype(jnp.bfloat16)
        return scaled

    def fold(product):
        return jnp.sum(product.reshape(-1, 8, HEAD), axis=0)

    def own_rows(n, head):
        return own[n, :, columns(head)]

    middle = heads // 2 - 1

    @pl.loop(0, heads)
    def _(step):
        for d in range(2):
            wait_if(receives[d], *(far_copy(step, d, m).wait_recv for m in range(2)))
        near_start(step, relays, True)

        @pl.when(step + AHEAD < heads)
        def _():
            for d in range(2):
                wait_if(sends[d], *(far_copy(step, d, m).wait_send for m in range(2)))
            far_start(step + AHEAD)
            near_start(step + AHEAD, direct, False)

        for n in range(2):

            @pl.when(step == 2 * n + 2)
            def _():
                learn(n)
                pass_on(n + 1)

        for stage in range(1, 3):

            @pl.when(step == middle + 1 + stage)
            def _():
                if stage == 2:
                    learn(2)
                share_start(stage, share_finish(stage - 1))

        for d in range(2):
            head = head_of(step, d)
            r1, r2 = own_rows(2 * d, head), own_rows(2 * d + 1, head)
            raw_s[d, 0] = dot_nt(r1, own_rows(2 - 2 * d, head))
            raw_s[d, 1] = dot_nt(r1, far[d, head, 0])
            gw_s[d, 0] = dot_nt(r2, own_rows(3 - 2 * d, head))
            gw_s[d, 1] = dot_nt(r2, far[d, head, 1])
        for d in range(2):
            head = head_of(step, d)
            scale = 0.5 * coeff * alpha_ref[head]
            total = jnp.zeros((8, HEAD), jnp.float32)
            for row in range(0, rows, STRIP):
                for column in range(0, rows, HEAD):
                    at = (pl.ds(row, STRIP), pl.ds(column, HEAD))
                    if row // HEAD == column // HEAD:
                        gap = column - row + lanes - sublanes
                        mine = gap <= 0 if d == 0 else gap >= 0
                        raw = jnp.where(mine, raw_s[d, 0, *at], raw_s[d, 1, *at])
                        gw = jnp.where(mine, gw_s[d, 0, *at], gw_s[d, 1, *at])
                        silu, grad = element(raw, gw, scale)
                        total += fold((weigh(d, 0, at, silu, grad) + weigh(d, 1, at, silu, grad)) * raw)
                    else:
                        segment = int((row < column) == (d == 0))
                        raw = raw_s[d, segment, *at]
                        silu, grad = element(raw, gw_s[d, segment, *at], scale)
                        total += fold(weigh(d, segment, at, silu, grad) * raw)
            da_ref[d, step] = total / alpha_ref[head]
            acc[d, 0] = dot_nn(w_s[d, 0], own_rows(3 - 2 * d, head)) + dot_nn(w_s[d, 1], far[d, head, 1])
            acc[d, 1] = dot_nn(gr_s[d, 0], own_rows(2 - 2 * d, head)) + dot_nn(gr_s[d, 1], far[d, head, 0])

        for d in range(2):
            wait_if(near_receives[d], *(near_copy(step, d, m, True).wait_recv for m in range(2)))
        for d in range(2):
            head = head_of(step, d)
            raw_s[d, 2] = dot_nt(own_rows(2 * d, head), near[d, head, 0])
            gw_s[d, 2] = dot_nt(own_rows(2 * d + 1, head), near[d, head, 1])
        for d in range(2):
            head = head_of(step, d)
            scale = 0.5 * coeff * alpha_ref[head]
            total = jnp.zeros((8, HEAD), jnp.float32)
            for row in range(0, rows, STRIP):
                for column in range(0, rows, HEAD):
                    at = (pl.ds(row, STRIP), pl.ds(column, HEAD))
                    raw = raw_s[d, 2, *at]
                    silu, grad = element(raw, gw_s[d, 2, *at], scale)
                    total += fold(weigh(d, 2, at, silu, grad) * raw)
            da_ref[d, step] += total / alpha_ref[head]
            first = acc[d, 0] + dot_nn(w_s[d, 2], near[d, head, 1])
            second = acc[d, 1] + dot_nn(gr_s[d, 2], near[d, head, 0])
            results[d][0][0, :, columns(head)] = first.astype(jnp.bfloat16)
            results[d][1][0, :, columns(head)] = second.astype(jnp.bfloat16)

        @pl.when(step == middle)
        def _():
            for d in range(2):
                half = pl.ds(d * (heads // 2), heads // 2)
                share[0, half] = jnp.sum(da_ref[d, pl.ds(0, heads // 2)], axis=1)
            share_start(0, share[0])

    @pl.loop(0, heads)
    def _(step):
        for d in range(2):
            wait_if(
                sends[d] & (step + AHEAD >= heads), *(far_copy(step, d, m).wait_send for m in range(2))
            )
            wait_if(near_sends[d], *(near_copy(step, d, m, True).wait_send for m in range(2)))

    sum_ref[...] = share_finish(2)
    for stage in range(3):
        for hop in range(1, LINE):
            share_copy(stage, hop, places[stage]).wait_send()


def shards(offsets, pairs, pair_count, queries, keys, values, cotangent, alpha):
    rows, width = queries.shape[1:]
    heads = alpha.shape[0]
    size = lax.axis_size("ctx")
    anywhere = pl.BlockSpec(memory_space=pl.ANY)

    def body(*refs):
        kernel(size, heads, offsets.shape[1] - 1, *refs)

    inputs = (offsets, alpha, queries, keys, values, cotangent)
    in_vmem = pltpu.VMEM((1, rows, width), jnp.bfloat16)
    *results, total = pl.pallas_call(
        body,
        out_shape=(in_vmem,) * 4 + (pltpu.VMEM((heads, HEAD), jnp.float32),),
        in_specs=[anywhere] * 6,
        out_specs=[pl.BlockSpec(memory_space=pltpu.VMEM)] * 5,
        scratch_shapes=[
            pltpu.SMEM(offsets.shape, jnp.int32),
            pltpu.SMEM(alpha.shape, jnp.float32),
            pltpu.VMEM((4, rows, width), jnp.bfloat16),
            pltpu.VMEM((2, heads, 2, rows, HEAD), jnp.bfloat16),
            pltpu.VMEM((2, heads, 2, rows, HEAD), jnp.bfloat16),
            pltpu.VMEM((2, heads, 8, HEAD), jnp.float32),
            pltpu.VMEM((3, heads, HEAD), jnp.float32),
            pltpu.VMEM((3, LINE, heads, HEAD), jnp.float32),
            pltpu.VMEM((2, 3, rows, rows), jnp.float32),
            pltpu.VMEM((2, 3, rows, rows), jnp.float32),
            pltpu.VMEM((2, 3, rows, rows), jnp.float32),
            pltpu.VMEM((2, 3, rows, rows), jnp.bfloat16),
            pltpu.VMEM((2, 3, rows, rows), jnp.bfloat16),
            pltpu.VMEM((2, 2, rows, HEAD), jnp.float32),
            pltpu.SemaphoreType.DMA((4, heads)),
            pltpu.SemaphoreType.DMA((2,)),
            pltpu.SemaphoreType.DMA((2, heads, 2)),
            pltpu.SemaphoreType.DMA((2, heads, 2)),
            pltpu.SemaphoreType.DMA((2, heads, 2)),
            pltpu.SemaphoreType.DMA((2, heads, 2)),
            pltpu.SemaphoreType.DMA((3, LINE)),
            pltpu.SemaphoreType.DMA((3, LINE)),
            pltpu.SemaphoreType.REGULAR((3,)),
        ],
        compiler_params=pltpu.CompilerParams(
            collective_id=0, has_side_effects=True, vmem_limit_bytes=40 * 1024 * 1024
        ),
        cost_estimate=pl.CostEstimate(
            flops=48 * heads * rows * rows * HEAD,
            bytes_accessed=8 * rows * width,
            transcendentals=4 * heads * rows * rows,
        ),
    )(*(pltpu.with_memory_space_constraint(array, pltpu.HBM) for array in inputs))
    return (*results, jnp.sum(total, axis=1))


def solution(mesh):
    return jax.shard_map(
        shards,
        mesh=mesh,
        in_specs=(
            P("rep", None),
            P("rep", "ctx", None),
            P("rep", "ctx"),
            P("rep", "ctx", None),
            P("rep", "ctx", None),
            P("rep", "ctx", None),
            P("rep", "ctx", None),
            P(),
        ),
        out_specs=(
            P("rep", "ctx", None),
            P("rep", "ctx", None),
            P("rep", "ctx", None),
            P("rep", "ctx", None),
            P(),
        ),
        check_vma=False,
    )
```

```python
import math

import jax
import jax.numpy as jnp
from jax import lax
from jax.experimental import pallas as pl
from jax.experimental.pallas import tpu as pltpu
from jax.sharding import PartitionSpec as P

WINDOW = 512
HEAD = 128
STRIP = 32
AHEAD = 3
LINE = 8
MESH = pl.DeviceIdType.MESH


def row_facts(offsets_ref, users, rows):
    start = jnp.zeros_like(rows)
    end = jnp.full_like(rows, 1 << 30)
    for user in range(users + 1):
        bound = offsets_ref[0, user]
        begun = rows >= bound
        start = jnp.where(begun, bound, start)
        end = jnp.where(begun, end, jnp.minimum(end, bound))
    length = jnp.minimum(end - start, WINDOW)
    return jnp.maximum(start, rows - (WINDOW - 1)), lax.rsqrt(length.astype(jnp.float32))


def fill_weights(offsets_ref, users, first, rows, weights):
    span = (rows, rows)
    down = lax.broadcasted_iota(jnp.int32, span, 0)
    across = lax.broadcasted_iota(jnp.int32, span, 1)
    lo, scale = row_facts(offsets_ref, users, first + lax.broadcasted_iota(jnp.int32, (rows, 1), 0))
    for segment, shift in ((0, 0), (1, -2 * rows), (2, -rows)):
        key = first + shift + across
        mask = (key >= lo) & (key <= first + down)
        weights[0, segment] = jnp.where(mask, scale, 0.0)
    for segment, shift in ((0, 0), (1, 2 * rows), (2, rows)):
        query = first + shift + lax.broadcasted_iota(jnp.int32, (1, rows), 1)
        lo, scale = row_facts(offsets_ref, users, query)
        key = first + down
        mask = (key >= lo) & (key <= query)
        weights[1, segment] = jnp.where(mask, scale, 0.0)


def dot_nt(left, right):
    return lax.dot_general(left, right, (((1,), (1,)), ((), ())), preferred_element_type=jnp.float32)


def dot_nn(left, right):
    return jnp.dot(left, right, preferred_element_type=jnp.float32)


def kernel(
    size,
    heads,
    users,
    offsets_hbm,
    alpha_hbm,
    q_hbm,
    k_hbm,
    v_hbm,
    g_hbm,
    out_ref,
    dq_ref,
    dk_ref,
    dv_ref,
    sum_ref,
    offsets_ref,
    alpha_ref,
    own,
    far,
    near,
    da_ref,
    share,
    gathered,
    weights,
    raw_s,
    gw_s,
    w_s,
    gr_s,
    acc,
    load_sem,
    fact_sem,
    far_send,
    far_recv,
    near_send,
    near_recv,
    share_send,
    share_recv,
    reached,
):
    rows = q_hbm.shape[1]
    coeff = 1.0 / math.sqrt(HEAD)
    me = lax.axis_index("ctx")
    core = lax.rem(me, 2)
    sibling = me + 1 - 2 * core
    ahead, behind = jnp.minimum(me + 2, size - 1), jnp.maximum(me - 2, 0)
    has_ahead, has_behind = me < size - 2, me >= 2
    arrays = (q_hbm, g_hbm, k_hbm, v_hbm)
    targets = (ahead, behind)
    sends, receives = (has_ahead, has_behind), (has_behind, has_ahead)
    direct = (core == 0, core == 1)
    relays = ((core == 1) & has_behind, (core == 0) & has_ahead)
    near_sends = (me != 1, me != size - 2)
    near_receives = (me != 0, me != size - 1)
    results = ((out_ref, dq_ref), (dv_ref, dk_ref))

    def head_of(step, d):
        return lax.rem(step + d * (heads // 2), heads)

    def columns(head):
        return pl.ds(pl.multiple_of(head * HEAD, HEAD), HEAD)

    def far_copy(step, d, m):
        head = head_of(step, d)
        return pltpu.make_async_remote_copy(
            src_ref=own.at[2 - 2 * d + m, :, columns(head)],
            dst_ref=far.at[d, head, m],
            send_sem=far_send.at[d, head, m],
            recv_sem=far_recv.at[d, head, m],
            device_id={"ctx": targets[d]},
            device_id_type=MESH,
        )

    def near_copy(step, d, m, forwarded):
        head = head_of(step, d)
        source = far.at[d, head, m] if forwarded else own.at[2 - 2 * d + m, :, columns(head)]
        return pltpu.make_async_remote_copy(
            src_ref=source,
            dst_ref=near.at[d, head, m],
            send_sem=near_send.at[d, head, m],
            recv_sem=near_recv.at[d, head, m],
            device_id={"ctx": sibling},
            device_id_type=MESH,
        )

    rep = lax.axis_index("rep")
    pair_x = rep * 2 + core
    y, z = lax.rem(me // 2, LINE), me // (2 * LINE)
    places = (pair_x, y, z)

    def member(stage, n):
        if stage == 0:
            return {"ctx": me - core + lax.rem(n, 2), "rep": n // 2}
        return {"ctx": me + (n - places[stage]) * (2 if stage == 1 else 2 * LINE), "rep": rep}

    def share_copy(stage, hop, slot):
        return pltpu.make_async_remote_copy(
            src_ref=share.at[stage],
            dst_ref=gathered.at[stage, slot],
            send_sem=share_send.at[stage, hop],
            recv_sem=share_recv.at[stage, slot],
            device_id=member(stage, lax.rem(places[stage] + hop, LINE)),
            device_id_type=MESH,
        )

    def share_start(stage, value):
        share[stage] = value
        gathered[stage, places[stage]] = value
        for hop in range(1, LINE):
            share_copy(stage, hop, places[stage]).start()

    def share_finish(stage):
        for hop in range(1, LINE):
            share_copy(stage, hop, lax.rem(places[stage] + hop, LINE)).wait_recv()
        return jnp.sum(gathered[stage], axis=0)

    def load(n, head):
        return pltpu.make_async_copy(
            arrays[n].at[0, :, columns(head)], own.at[n, :, columns(head)], load_sem.at[n, head]
        )

    def sent_at(step):
        return [(2 - 2 * d + m, head_of(step, d)) for d in range(2) for m in range(2)]

    facts = [
        pltpu.make_async_copy(offsets_hbm, offsets_ref, fact_sem.at[0]),
        pltpu.make_async_copy(alpha_hbm, alpha_ref, fact_sem.at[1]),
    ]

    @pl.loop(0, heads)
    def _(step):
        for piece in sent_at(step):
            load(*piece).start()

    for copy in facts:
        copy.start()
    def far_start(step):
        for first in range(2):
            for m in range(2):
                for d in (first, 1 - first):

                    @pl.when((core == first) & sends[d])
                    def _():
                        far_copy(step, d, m).start()

    def near_start(step, conditions, forwarded):
        for d in range(2):

            @pl.when(conditions[d])
            def _():
                for m in range(2):
                    near_copy(step, d, m, forwarded).start()

    def wait_if(condition, *waits):
        @pl.when(condition)
        def _():
            for wait in waits:
                wait()

    barrier = pltpu.get_barrier_semaphore()

    def along_z(distance):
        inside = z + distance < LINE if distance > 0 else z + distance >= 0
        return inside, {"ctx": jnp.clip(me + 2 * LINE * distance, 0, size - 1)}

    def count(conditions):
        return sum(condition.astype(jnp.int32) for condition in conditions)

    greeted = [(has_ahead, {"ctx": ahead}), (has_behind, {"ctx": behind}), along_z(1), along_z(-1)]
    for exists, device in greeted:

        @pl.when(exists)
        def _():
            pl.semaphore_signal(barrier, inc=1, device_id=device, device_id_type=MESH)

    pl.semaphore_signal(barrier, inc=1, device_id={"ctx": sibling}, device_id_type=MESH)
    for stage in range(2):
        for hop in range(1, LINE):
            other = lax.rem(places[stage] + hop, LINE)
            pl.semaphore_signal(barrier, inc=1, device_id=member(stage, other), device_id_type=MESH)
    pl.semaphore_wait(barrier, 1 + 2 * (LINE - 1) + count([exists for exists, _ in greeted]))

    for step in range(AHEAD):
        for piece in sent_at(step):
            load(*piece).wait()
        far_start(step)
    for step in range(AHEAD):
        near_start(step, direct, False)

    def pass_on(n):
        for distance in (1 << n, -(1 << n)):
            exists, device = along_z(distance)

            @pl.when(exists)
            def _():
                pl.semaphore_signal(reached.at[n], inc=1, device_id=device, device_id_type=MESH)

    def learn(n):
        pl.semaphore_wait(reached.at[n], count([along_z(1 << n)[0], along_z(-(1 << n))[0]]))

    pass_on(0)
    for d in range(2):

        @pl.when(jnp.logical_not(receives[d]))
        def _():
            far[d] = jnp.zeros(far.shape[1:], far.dtype)

        @pl.when(jnp.logical_not(near_receives[d]))
        def _():
            near[d] = jnp.zeros(near.shape[1:], near.dtype)

    for copy in facts:
        copy.wait()
    fill_weights(offsets_ref, users, me * rows, rows, weights)
    lanes = lax.broadcasted_iota(jnp.int32, (STRIP, HEAD), 1)
    sublanes = lax.broadcasted_iota(jnp.int32, (STRIP, HEAD), 0)
    w_s[...] = jnp.zeros_like(w_s)
    gr_s[...] = jnp.zeros_like(gr_s)
    @pl.loop(AHEAD, heads)
    def _(step):
        for piece in sent_at(step):
            load(*piece).wait()

    def element(raw, gw, scale):
        half = raw * scale
        tanh = jnp.tanh(half)
        twice = 1.0 + tanh
        silu = half * twice
        return silu, gw * scale * (twice + silu * (1.0 - tanh))

    def weigh(d, segment, at, silu, grad):
        weight = weights[d, segment, *at]
        w_s[d, segment, *at] = (silu * weight).astype(jnp.bfloat16)
        scaled = grad * weight
        gr_s[d, segment, *at] = scaled.astype(jnp.bfloat16)
        return scaled

    def fold(product):
        return jnp.sum(product.reshape(-1, 8, HEAD), axis=0)

    def own_rows(n, head):
        return own[n, :, columns(head)]

    middle = heads // 2 - 1

    def send_next(step):
        for d in range(2):
            wait_if(sends[d], *(far_copy(step, d, m).wait_send for m in range(2)))
        far_start(step + AHEAD)
        near_start(step + AHEAD, direct, False)

    @pl.loop(0, heads)
    def _(step):
        for d in range(2):
            wait_if(receives[d], *(far_copy(step, d, m).wait_recv for m in range(2)))
        near_start(step, relays, True)

        @pl.when(step < middle)
        def _():
            send_next(step)

        for n in range(2):

            @pl.when(step == 2 * n + 2)
            def _():
                learn(n)
                pass_on(n + 1)

        for stage in range(1, 3):

            @pl.when(step == middle + 1 + stage)
            def _():
                if stage == 2:
                    learn(2)
                share_start(stage, share_finish(stage - 1))
                if stage == 2:
                    send_next(heads - 1 - AHEAD)

        for d in range(2):
            head = head_of(step, d)
            r1, r2 = own_rows(2 * d, head), own_rows(2 * d + 1, head)
            raw_s[d, 0] = dot_nt(r1, own_rows(2 - 2 * d, head))
            raw_s[d, 1] = dot_nt(r1, far[d, head, 0])
            gw_s[d, 0] = dot_nt(r2, own_rows(3 - 2 * d, head))
            gw_s[d, 1] = dot_nt(r2, far[d, head, 1])
        for d in range(2):
            head = head_of(step, d)
            scale = 0.5 * coeff * alpha_ref[head]
            total = jnp.zeros((8, HEAD), jnp.float32)
            for row in range(0, rows, STRIP):
                for column in range(0, rows, HEAD):
                    at = (pl.ds(row, STRIP), pl.ds(column, HEAD))
                    if row // HEAD == column // HEAD:
                        gap = column - row + lanes - sublanes
                        mine = gap <= 0 if d == 0 else gap >= 0
                        raw = jnp.where(mine, raw_s[d, 0, *at], raw_s[d, 1, *at])
                        gw = jnp.where(mine, gw_s[d, 0, *at], gw_s[d, 1, *at])
                        silu, grad = element(raw, gw, scale)
                        total += fold((weigh(d, 0, at, silu, grad) + weigh(d, 1, at, silu, grad)) * raw)
                    else:
                        segment = int((row < column) == (d == 0))
                        raw = raw_s[d, segment, *at]
                        silu, grad = element(raw, gw_s[d, segment, *at], scale)
                        total += fold(weigh(d, segment, at, silu, grad) * raw)
            da_ref[d, step] = total / alpha_ref[head]
            acc[d, 0] = dot_nn(w_s[d, 0], own_rows(3 - 2 * d, head)) + dot_nn(w_s[d, 1], far[d, head, 1])
            acc[d, 1] = dot_nn(gr_s[d, 0], own_rows(2 - 2 * d, head)) + dot_nn(gr_s[d, 1], far[d, head, 0])

        for d in range(2):
            wait_if(near_receives[d], *(near_copy(step, d, m, True).wait_recv for m in range(2)))
        for d in range(2):
            head = head_of(step, d)
            raw_s[d, 2] = dot_nt(own_rows(2 * d, head), near[d, head, 0])
            gw_s[d, 2] = dot_nt(own_rows(2 * d + 1, head), near[d, head, 1])
        for d in range(2):
            head = head_of(step, d)
            scale = 0.5 * coeff * alpha_ref[head]
            total = jnp.zeros((8, HEAD), jnp.float32)
            for row in range(0, rows, STRIP):
                for column in range(0, rows, HEAD):
                    at = (pl.ds(row, STRIP), pl.ds(column, HEAD))
                    raw = raw_s[d, 2, *at]
                    silu, grad = element(raw, gw_s[d, 2, *at], scale)
                    total += fold(weigh(d, 2, at, silu, grad) * raw)
            da_ref[d, step] += total / alpha_ref[head]
            first = acc[d, 0] + dot_nn(w_s[d, 2], near[d, head, 1])
            second = acc[d, 1] + dot_nn(gr_s[d, 2], near[d, head, 0])
            results[d][0][0, :, columns(head)] = first.astype(jnp.bfloat16)
            results[d][1][0, :, columns(head)] = second.astype(jnp.bfloat16)

        @pl.when(step == middle)
        def _():
            for d in range(2):
                half = pl.ds(d * (heads // 2), heads // 2)
                share[0, half] = jnp.sum(da_ref[d, pl.ds(0, heads // 2)], axis=1)
            share_start(0, share[0])
            send_next(middle)

    @pl.loop(0, heads)
    def _(step):
        for d in range(2):
            wait_if(
                sends[d] & (step + AHEAD >= heads), *(far_copy(step, d, m).wait_send for m in range(2))
            )
            wait_if(near_sends[d], *(near_copy(step, d, m, True).wait_send for m in range(2)))

    sum_ref[...] = share_finish(2)
    for stage in range(3):
        for hop in range(1, LINE):
            share_copy(stage, hop, places[stage]).wait_send()


def shards(offsets, pairs, pair_count, queries, keys, values, cotangent, alpha):
    rows, width = queries.shape[1:]
    heads = alpha.shape[0]
    size = lax.axis_size("ctx")
    anywhere = pl.BlockSpec(memory_space=pl.ANY)

    def body(*refs):
        kernel(size, heads, offsets.shape[1] - 1, *refs)

    inputs = (offsets, alpha, queries, keys, values, cotangent)
    in_vmem = pltpu.VMEM((1, rows, width), jnp.bfloat16)
    *results, total = pl.pallas_call(
        body,
        out_shape=(in_vmem,) * 4 + (pltpu.VMEM((heads, HEAD), jnp.float32),),
        in_specs=[anywhere] * 6,
        out_specs=[pl.BlockSpec(memory_space=pltpu.VMEM)] * 5,
        scratch_shapes=[
            pltpu.SMEM(offsets.shape, jnp.int32),
            pltpu.SMEM(alpha.shape, jnp.float32),
            pltpu.VMEM((4, rows, width), jnp.bfloat16),
            pltpu.VMEM((2, heads, 2, rows, HEAD), jnp.bfloat16),
            pltpu.VMEM((2, heads, 2, rows, HEAD), jnp.bfloat16),
            pltpu.VMEM((2, heads, 8, HEAD), jnp.float32),
            pltpu.VMEM((3, heads, HEAD), jnp.float32),
            pltpu.VMEM((3, LINE, heads, HEAD), jnp.float32),
            pltpu.VMEM((2, 3, rows, rows), jnp.float32),
            pltpu.VMEM((2, 3, rows, rows), jnp.float32),
            pltpu.VMEM((2, 3, rows, rows), jnp.float32),
            pltpu.VMEM((2, 3, rows, rows), jnp.bfloat16),
            pltpu.VMEM((2, 3, rows, rows), jnp.bfloat16),
            pltpu.VMEM((2, 2, rows, HEAD), jnp.float32),
            pltpu.SemaphoreType.DMA((4, heads)),
            pltpu.SemaphoreType.DMA((2,)),
            pltpu.SemaphoreType.DMA((2, heads, 2)),
            pltpu.SemaphoreType.DMA((2, heads, 2)),
            pltpu.SemaphoreType.DMA((2, heads, 2)),
            pltpu.SemaphoreType.DMA((2, heads, 2)),
            pltpu.SemaphoreType.DMA((3, LINE)),
            pltpu.SemaphoreType.DMA((3, LINE)),
            pltpu.SemaphoreType.REGULAR((3,)),
        ],
        compiler_params=pltpu.CompilerParams(
            collective_id=0, has_side_effects=True, vmem_limit_bytes=40 * 1024 * 1024
        ),
        cost_estimate=pl.CostEstimate(
            flops=48 * heads * rows * rows * HEAD,
            bytes_accessed=8 * rows * width,
            transcendentals=4 * heads * rows * rows,
        ),
    )(*(pltpu.with_memory_space_constraint(array, pltpu.HBM) for array in inputs))
    return (*results, jnp.sum(total, axis=1))


def solution(mesh):
    return jax.shard_map(
        shards,
        mesh=mesh,
        in_specs=(
            P("rep", None),
            P("rep", "ctx", None),
            P("rep", "ctx"),
            P("rep", "ctx", None),
            P("rep", "ctx", None),
            P("rep", "ctx", None),
            P("rep", "ctx", None),
            P(),
        ),
        out_specs=(
            P("rep", "ctx", None),
            P("rep", "ctx", None),
            P("rep", "ctx", None),
            P("rep", "ctx", None),
            P(),
        ),
        check_vma=False,
    )
```

```python
import math

import jax
import jax.numpy as jnp
from jax import lax
from jax.experimental import pallas as pl
from jax.experimental.pallas import tpu as pltpu
from jax.sharding import PartitionSpec as P

WINDOW = 512
HEAD = 128
STRIP = 32
AHEAD = 4
LINE = 8
MESH = pl.DeviceIdType.MESH


def row_facts(offsets_ref, users, rows):
    start = jnp.zeros_like(rows)
    end = jnp.full_like(rows, 1 << 30)
    for user in range(users + 1):
        bound = offsets_ref[0, user]
        begun = rows >= bound
        start = jnp.where(begun, bound, start)
        end = jnp.where(begun, end, jnp.minimum(end, bound))
    length = jnp.minimum(end - start, WINDOW)
    return jnp.maximum(start, rows - (WINDOW - 1)), lax.rsqrt(length.astype(jnp.float32))


def fill_weights(offsets_ref, users, first, rows, weights):
    span = (rows, rows)
    down = lax.broadcasted_iota(jnp.int32, span, 0)
    across = lax.broadcasted_iota(jnp.int32, span, 1)
    lo, scale = row_facts(offsets_ref, users, first + lax.broadcasted_iota(jnp.int32, (rows, 1), 0))
    for segment, shift in ((0, 0), (1, -2 * rows), (2, -rows)):
        key = first + shift + across
        mask = (key >= lo) & (key <= first + down)
        weights[0, segment] = jnp.where(mask, scale, 0.0)
    for segment, shift in ((0, 0), (1, 2 * rows), (2, rows)):
        query = first + shift + lax.broadcasted_iota(jnp.int32, (1, rows), 1)
        lo, scale = row_facts(offsets_ref, users, query)
        key = first + down
        mask = (key >= lo) & (key <= query)
        weights[1, segment] = jnp.where(mask, scale, 0.0)


def dot_nt(left, right):
    return lax.dot_general(left, right, (((1,), (1,)), ((), ())), preferred_element_type=jnp.float32)


def dot_nn(left, right):
    return jnp.dot(left, right, preferred_element_type=jnp.float32)


def kernel(
    size,
    heads,
    users,
    offsets_hbm,
    alpha_hbm,
    q_hbm,
    k_hbm,
    v_hbm,
    g_hbm,
    out_ref,
    dq_ref,
    dk_ref,
    dv_ref,
    sum_ref,
    offsets_ref,
    alpha_ref,
    own,
    far,
    near,
    da_ref,
    share,
    gathered,
    weights,
    raw_s,
    gw_s,
    w_s,
    gr_s,
    acc,
    load_sem,
    fact_sem,
    far_send,
    far_recv,
    near_send,
    near_recv,
    share_send,
    share_recv,
    reached,
):
    rows = q_hbm.shape[1]
    coeff = 1.0 / math.sqrt(HEAD)
    me = lax.axis_index("ctx")
    core = lax.rem(me, 2)
    sibling = me + 1 - 2 * core
    ahead, behind = jnp.minimum(me + 2, size - 1), jnp.maximum(me - 2, 0)
    has_ahead, has_behind = me < size - 2, me >= 2
    arrays = (q_hbm, g_hbm, k_hbm, v_hbm)
    targets = (ahead, behind)
    sends, receives = (has_ahead, has_behind), (has_behind, has_ahead)
    direct = (core == 0, core == 1)
    relays = ((core == 1) & has_behind, (core == 0) & has_ahead)
    near_sends = (me != 1, me != size - 2)
    near_receives = (me != 0, me != size - 1)
    results = ((out_ref, dq_ref), (dv_ref, dk_ref))

    def head_of(step, d):
        return lax.rem(step + d * (heads // 2), heads)

    def columns(head):
        return pl.ds(pl.multiple_of(head * HEAD, HEAD), HEAD)

    def far_copy(step, d, m):
        head = head_of(step, d)
        return pltpu.make_async_remote_copy(
            src_ref=own.at[2 - 2 * d + m, :, columns(head)],
            dst_ref=far.at[d, head, m],
            send_sem=far_send.at[d, head, m],
            recv_sem=far_recv.at[d, head, m],
            device_id={"ctx": targets[d]},
            device_id_type=MESH,
        )

    def near_copy(step, d, m, forwarded):
        head = head_of(step, d)
        source = far.at[d, head, m] if forwarded else own.at[2 - 2 * d + m, :, columns(head)]
        return pltpu.make_async_remote_copy(
            src_ref=source,
            dst_ref=near.at[d, head, m],
            send_sem=near_send.at[d, head, m],
            recv_sem=near_recv.at[d, head, m],
            device_id={"ctx": sibling},
            device_id_type=MESH,
        )

    rep = lax.axis_index("rep")
    pair_x = rep * 2 + core
    y, z = lax.rem(me // 2, LINE), me // (2 * LINE)
    places = (pair_x, y, z)

    def member(stage, n):
        if stage == 0:
            return {"ctx": me - core + lax.rem(n, 2), "rep": n // 2}
        return {"ctx": me + (n - places[stage]) * (2 if stage == 1 else 2 * LINE), "rep": rep}

    def share_copy(stage, hop, slot):
        return pltpu.make_async_remote_copy(
            src_ref=share.at[stage],
            dst_ref=gathered.at[stage, slot],
            send_sem=share_send.at[stage, hop],
            recv_sem=share_recv.at[stage, slot],
            device_id=member(stage, lax.rem(places[stage] + hop, LINE)),
            device_id_type=MESH,
        )

    def share_start(stage, value):
        share[stage] = value
        gathered[stage, places[stage]] = value
        for hop in range(1, LINE):
            share_copy(stage, hop, places[stage]).start()

    def share_finish(stage):
        for hop in range(1, LINE):
            share_copy(stage, hop, lax.rem(places[stage] + hop, LINE)).wait_recv()
        return jnp.sum(gathered[stage], axis=0)

    def load(n, head):
        return pltpu.make_async_copy(
            arrays[n].at[0, :, columns(head)], own.at[n, :, columns(head)], load_sem.at[n, head]
        )

    def sent_at(step):
        return [(2 - 2 * d + m, head_of(step, d)) for d in range(2) for m in range(2)]

    facts = [
        pltpu.make_async_copy(offsets_hbm, offsets_ref, fact_sem.at[0]),
        pltpu.make_async_copy(alpha_hbm, alpha_ref, fact_sem.at[1]),
    ]

    @pl.loop(0, heads)
    def _(step):
        for piece in sent_at(step):
            load(*piece).start()

    for copy in facts:
        copy.start()
    def far_start(step):
        for first in range(2):
            for m in range(2):
                for d in (first, 1 - first):

                    @pl.when((core == first) & sends[d])
                    def _():
                        far_copy(step, d, m).start()

    def near_start(step, conditions, forwarded):
        for d in range(2):

            @pl.when(conditions[d])
            def _():
                for m in range(2):
                    near_copy(step, d, m, forwarded).start()

    def wait_if(condition, *waits):
        @pl.when(condition)
        def _():
            for wait in waits:
                wait()

    barrier = pltpu.get_barrier_semaphore()

    def along_z(distance):
        inside = z + distance < LINE if distance > 0 else z + distance >= 0
        return inside, {"ctx": jnp.clip(me + 2 * LINE * distance, 0, size - 1)}

    def count(conditions):
        return sum(condition.astype(jnp.int32) for condition in conditions)

    greeted = [(has_ahead, {"ctx": ahead}), (has_behind, {"ctx": behind}), along_z(1), along_z(-1)]
    for exists, device in greeted:

        @pl.when(exists)
        def _():
            pl.semaphore_signal(barrier, inc=1, device_id=device, device_id_type=MESH)

    pl.semaphore_signal(barrier, inc=1, device_id={"ctx": sibling}, device_id_type=MESH)
    for stage in range(2):
        for hop in range(1, LINE):
            other = lax.rem(places[stage] + hop, LINE)
            pl.semaphore_signal(barrier, inc=1, device_id=member(stage, other), device_id_type=MESH)
    pl.semaphore_wait(barrier, 1 + 2 * (LINE - 1) + count([exists for exists, _ in greeted]))

    for step in range(AHEAD):
        for piece in sent_at(step):
            load(*piece).wait()
        far_start(step)
    for step in range(AHEAD):
        near_start(step, direct, False)

    def pass_on(n):
        for distance in (1 << n, -(1 << n)):
            exists, device = along_z(distance)

            @pl.when(exists)
            def _():
                pl.semaphore_signal(reached.at[n], inc=1, device_id=device, device_id_type=MESH)

    def learn(n):
        pl.semaphore_wait(reached.at[n], count([along_z(1 << n)[0], along_z(-(1 << n))[0]]))

    pass_on(0)
    for d in range(2):

        @pl.when(jnp.logical_not(receives[d]))
        def _():
            far[d] = jnp.zeros(far.shape[1:], far.dtype)

        @pl.when(jnp.logical_not(near_receives[d]))
        def _():
            near[d] = jnp.zeros(near.shape[1:], near.dtype)

    for copy in facts:
        copy.wait()
    fill_weights(offsets_ref, users, me * rows, rows, weights)
    lanes = lax.broadcasted_iota(jnp.int32, (STRIP, HEAD), 1)
    sublanes = lax.broadcasted_iota(jnp.int32, (STRIP, HEAD), 0)
    w_s[...] = jnp.zeros_like(w_s)
    gr_s[...] = jnp.zeros_like(gr_s)
    @pl.loop(AHEAD, heads)
    def _(step):
        for piece in sent_at(step):
            load(*piece).wait()

    def element(raw, gw, scale):
        half = raw * scale
        tanh = jnp.tanh(half)
        twice = 1.0 + tanh
        silu = half * twice
        return silu, gw * scale * (twice + silu * (1.0 - tanh))

    def weigh(d, segment, at, silu, grad):
        weight = weights[d, segment, *at]
        w_s[d, segment, *at] = (silu * weight).astype(jnp.bfloat16)
        scaled = grad * weight
        gr_s[d, segment, *at] = scaled.astype(jnp.bfloat16)
        return scaled

    def fold(product):
        return jnp.sum(product.reshape(-1, 8, HEAD), axis=0)

    def own_rows(n, head):
        return own[n, :, columns(head)]

    middle = heads // 2 - 1

    @pl.loop(0, heads)
    def _(step):
        for d in range(2):
            wait_if(receives[d], *(far_copy(step, d, m).wait_recv for m in range(2)))
        near_start(step, relays, True)

        @pl.when(step + AHEAD < heads)
        def _():
            for d in range(2):
                wait_if(sends[d], *(far_copy(step, d, m).wait_send for m in range(2)))
            far_start(step + AHEAD)
            near_start(step + AHEAD, direct, False)

        for n in range(2):

            @pl.when(step == 2 * n + 2)
            def _():
                learn(n)
                pass_on(n + 1)

        for stage in range(1, 3):

            @pl.when(step == middle + 1 + stage)
            def _():
                if stage == 2:
                    learn(2)
                share_start(stage, share_finish(stage - 1))

        for d in range(2):
            head = head_of(step, d)
            r1, r2 = own_rows(2 * d, head), own_rows(2 * d + 1, head)
            raw_s[d, 0] = dot_nt(r1, own_rows(2 - 2 * d, head))
            raw_s[d, 1] = dot_nt(r1, far[d, head, 0])
            gw_s[d, 0] = dot_nt(r2, own_rows(3 - 2 * d, head))
            gw_s[d, 1] = dot_nt(r2, far[d, head, 1])
        for d in range(2):
            head = head_of(step, d)
            scale = 0.5 * coeff * alpha_ref[head]
            total = jnp.zeros((8, HEAD), jnp.float32)
            for row in range(0, rows, STRIP):
                for column in range(0, rows, HEAD):
                    at = (pl.ds(row, STRIP), pl.ds(column, HEAD))
                    if row // HEAD == column // HEAD:
                        gap = column - row + lanes - sublanes
                        mine = gap <= 0 if d == 0 else gap >= 0
                        raw = jnp.where(mine, raw_s[d, 0, *at], raw_s[d, 1, *at])
                        gw = jnp.where(mine, gw_s[d, 0, *at], gw_s[d, 1, *at])
                        silu, grad = element(raw, gw, scale)
                        total += fold((weigh(d, 0, at, silu, grad) + weigh(d, 1, at, silu, grad)) * raw)
                    else:
                        segment = int((row < column) == (d == 0))
                        raw = raw_s[d, segment, *at]
                        silu, grad = element(raw, gw_s[d, segment, *at], scale)
                        total += fold(weigh(d, segment, at, silu, grad) * raw)
            da_ref[d, step] = total / alpha_ref[head]
            acc[d, 0] = dot_nn(w_s[d, 0], own_rows(3 - 2 * d, head)) + dot_nn(w_s[d, 1], far[d, head, 1])
            acc[d, 1] = dot_nn(gr_s[d, 0], own_rows(2 - 2 * d, head)) + dot_nn(gr_s[d, 1], far[d, head, 0])

        for d in range(2):
            wait_if(near_receives[d], *(near_copy(step, d, m, True).wait_recv for m in range(2)))
        for d in range(2):
            head = head_of(step, d)
            raw_s[d, 2] = dot_nt(own_rows(2 * d, head), near[d, head, 0])
            gw_s[d, 2] = dot_nt(own_rows(2 * d + 1, head), near[d, head, 1])
        for d in range(2):
            head = head_of(step, d)
            scale = 0.5 * coeff * alpha_ref[head]
            total = jnp.zeros((8, HEAD), jnp.float32)
            for row in range(0, rows, STRIP):
                for column in range(0, rows, HEAD):
                    at = (pl.ds(row, STRIP), pl.ds(column, HEAD))
                    raw = raw_s[d, 2, *at]
                    silu, grad = element(raw, gw_s[d, 2, *at], scale)
                    total += fold(weigh(d, 2, at, silu, grad) * raw)
            da_ref[d, step] += total / alpha_ref[head]
            first = acc[d, 0] + dot_nn(w_s[d, 2], near[d, head, 1])
            second = acc[d, 1] + dot_nn(gr_s[d, 2], near[d, head, 0])
            results[d][0][0, :, columns(head)] = first.astype(jnp.bfloat16)
            results[d][1][0, :, columns(head)] = second.astype(jnp.bfloat16)

        @pl.when(step == middle)
        def _():
            for d in range(2):
                half = pl.ds(d * (heads // 2), heads // 2)
                share[0, half] = jnp.sum(da_ref[d, pl.ds(0, heads // 2)], axis=1)
            share_start(0, share[0])

    @pl.loop(0, heads)
    def _(step):
        for d in range(2):
            wait_if(
                sends[d] & (step + AHEAD >= heads), *(far_copy(step, d, m).wait_send for m in range(2))
            )
            wait_if(near_sends[d], *(near_copy(step, d, m, True).wait_send for m in range(2)))

    sum_ref[...] = share_finish(2)
    for stage in range(3):
        for hop in range(1, LINE):
            share_copy(stage, hop, places[stage]).wait_send()


def shards(offsets, pairs, pair_count, queries, keys, values, cotangent, alpha):
    rows, width = queries.shape[1:]
    heads = alpha.shape[0]
    size = lax.axis_size("ctx")
    anywhere = pl.BlockSpec(memory_space=pl.ANY)

    def body(*refs):
        kernel(size, heads, offsets.shape[1] - 1, *refs)

    inputs = (offsets, alpha, queries, keys, values, cotangent)
    in_vmem = pltpu.VMEM((1, rows, width), jnp.bfloat16)
    *results, total = pl.pallas_call(
        body,
        out_shape=(in_vmem,) * 4 + (pltpu.VMEM((heads, HEAD), jnp.float32),),
        in_specs=[anywhere] * 6,
        out_specs=[pl.BlockSpec(memory_space=pltpu.VMEM)] * 5,
        scratch_shapes=[
            pltpu.SMEM(offsets.shape, jnp.int32),
            pltpu.SMEM(alpha.shape, jnp.float32),
            pltpu.VMEM((4, rows, width), jnp.bfloat16),
            pltpu.VMEM((2, heads, 2, rows, HEAD), jnp.bfloat16),
            pltpu.VMEM((2, heads, 2, rows, HEAD), jnp.bfloat16),
            pltpu.VMEM((2, heads, 8, HEAD), jnp.float32),
            pltpu.VMEM((3, heads, HEAD), jnp.float32),
            pltpu.VMEM((3, LINE, heads, HEAD), jnp.float32),
            pltpu.VMEM((2, 3, rows, rows), jnp.float32),
            pltpu.VMEM((2, 3, rows, rows), jnp.float32),
            pltpu.VMEM((2, 3, rows, rows), jnp.float32),
            pltpu.VMEM((2, 3, rows, rows), jnp.bfloat16),
            pltpu.VMEM((2, 3, rows, rows), jnp.bfloat16),
            pltpu.VMEM((2, 2, rows, HEAD), jnp.float32),
            pltpu.SemaphoreType.DMA((4, heads)),
            pltpu.SemaphoreType.DMA((2,)),
            pltpu.SemaphoreType.DMA((2, heads, 2)),
            pltpu.SemaphoreType.DMA((2, heads, 2)),
            pltpu.SemaphoreType.DMA((2, heads, 2)),
            pltpu.SemaphoreType.DMA((2, heads, 2)),
            pltpu.SemaphoreType.DMA((3, LINE)),
            pltpu.SemaphoreType.DMA((3, LINE)),
            pltpu.SemaphoreType.REGULAR((3,)),
        ],
        compiler_params=pltpu.CompilerParams(
            collective_id=0, has_side_effects=True, vmem_limit_bytes=40 * 1024 * 1024
        ),
        cost_estimate=pl.CostEstimate(
            flops=48 * heads * rows * rows * HEAD,
            bytes_accessed=8 * rows * width,
            transcendentals=4 * heads * rows * rows,
        ),
    )(*(pltpu.with_memory_space_constraint(array, pltpu.HBM) for array in inputs))
    return (*results, jnp.sum(total, axis=1))


def solution(mesh):
    return jax.shard_map(
        shards,
        mesh=mesh,
        in_specs=(
            P("rep", None),
            P("rep", "ctx", None),
            P("rep", "ctx"),
            P("rep", "ctx", None),
            P("rep", "ctx", None),
            P("rep", "ctx", None),
            P("rep", "ctx", None),
            P(),
        ),
        out_specs=(
            P("rep", "ctx", None),
            P("rep", "ctx", None),
            P("rep", "ctx", None),
            P("rep", "ctx", None),
            P(),
        ),
        check_vma=False,
    )
```
